128 devices in a mesh: gx: 8 (over z_lo, y), gy: 8 (over z_hi, x), grid: 2 (over core).
Axes of the slice: x: 4, y: 4, z: 4 (z_hi: 2, z_lo: 2; z = z_hi * 2 + z_lo), core: 2. Of those that a mesh axis runs over, the one named last changes fastest.
Arguments:
- fine_now: float32 [3, 16, 512, 4096], P(None, 'grid', 'gx', 'gy'), may hold values from -6 to 6
- fine_prev: float32 [3, 16, 512, 4096], P(None, 'grid', 'gx', 'gy'), may hold values from -6 to 6
- fine_mu: float32 [16, 512, 4096], P('grid', 'gx', 'gy'), may hold values from 0.3 to 1
- fine_lam: float32 [16, 512, 4096], P('grid', 'gx', 'gy'), may hold values from 0.3 to 1
- fine_rho: float32 [16, 512, 4096], P('grid', 'gx', 'gy'), may hold values from 1 to 2
- fine_stretch: float32 [16, 512, 4096], P('grid', 'gx', 'gy'), may hold values from 0.7 to 1.4
- coarse_now: float32 [3, 16, 256, 2048], P(None, 'grid', 'gx', 'gy'), may hold values from -6 to 6
- coarse_prev: float32 [3, 16, 256, 2048], P(None, 'grid', 'gx', 'gy'), may hold values from -6 to 6
- coarse_mu: float32 [16, 256, 2048], P('grid', 'gx', 'gy'), may hold values from 1.5 to 4
- coarse_lam: float32 [16, 256, 2048], P('grid', 'gx', 'gy'), may hold values from 1 to 4
- coarse_rho: float32 [16, 256, 2048], P('grid', 'gx', 'gy'), may hold values from 1 to 2
- fine_ghost: float32 [3, 512, 4096], P(None, 'gx', 'gy'), may hold values from -6 to 6
- coarse_ghost: float32 [3, 256, 2048], P(None, 'gx', 'gy'), may hold values from -6 to 6
Outputs:
- fine_next: float32 [3, 16, 512, 4096], P(None, 'grid', 'gx', 'gy')
- coarse_next: float32 [3, 16, 256, 2048], P(None, 'grid', 'gx', 'gy')
The draws below stay inside these ranges and needn't reach their ends.
All inputs are finite; a program needn't handle non-finite values.
Results may differ from the reference program's by a relative error of at most 0.00002.
Values sent between devices are 32-bit elements; how exact they have to be, the bound alone decides.
No kernel may reach another device: no remote copies, remote signals or barrier semaphores. Data moves between devices by JAX's collectives and lax.ppermute only.
A program may use at most 128 MiB of HBM per device.

```python
import math
import jax
import jax.numpy as jnp

ZF = 16
ZC = 16
SWEEPS = 3
NXF = 512
NYF = 4096
NXC = 256
NYC = 2048


def steps_of(key, shape, split, least, top_value):
    level = 1.0
    for axis_at, shards_of in split:
        draws = jax.random.uniform(jax.random.fold_in(jax.random.fold_in(key, 6), axis_at), (shards_of,), jnp.float32, least / len(split), top_value / len(split))
        level = level * jnp.repeat(jnp.exp(draws), shape[axis_at] // shards_of).reshape((-1,) + (1,) * (len(shape) - 1 - axis_at))
    return level


def gaussian(rng, shape, deviation, limit, shards=(), kind=jnp.bfloat16):
    factor_of = steps_of(rng, shape, shards, -0.22, 0.18) if shards else 1.0
    drawn = jax.random.normal(rng, shape, jnp.float32) * deviation * factor_of
    return jnp.minimum(jnp.maximum(drawn, -limit), limit).astype(kind)


def setup_inputs(seed: int = 0) -> dict:
    key_list = jax.random.split(jax.random.key(seed), 14)
    fine_now = gaussian(key_list[0], (3, ZF, NXF, NYF), 1.0, 6.0, ((1, 2), (2, 8), (3, 8)), jnp.float32)
    fine_prev = gaussian(key_list[1], (3, ZF, NXF, NYF), 1.0, 6.0, ((1, 2), (2, 8), (3, 8)), jnp.float32)
    fine_mu = jnp.clip(0.3 + 0.7 * jax.random.uniform(key_list[2], (ZF, NXF, NYF), jnp.float32) ** steps_of(key_list[2], (ZF, NXF, NYF), ((0, 2), (1, 8), (2, 8)), -0.2, 0.2), 0.3, 1.0)
    fine_lam = jnp.clip(0.3 + 0.7 * jax.random.uniform(key_list[3], (ZF, NXF, NYF), jnp.float32) ** steps_of(key_list[3], (ZF, NXF, NYF), ((0, 2), (1, 8), (2, 8)), -0.2, 0.2), 0.3, 1.0)
    fine_rho = jnp.clip(1.0 + 1.0 * jax.random.uniform(key_list[4], (ZF, NXF, NYF), jnp.float32) ** steps_of(key_list[4], (ZF, NXF, NYF), ((0, 2), (1, 8), (2, 8)), -0.2, 0.2), 1.0, 2.0)
    fine_stretch = jnp.clip(jnp.exp(math.log(1.4) - 0.6931472 * jax.random.uniform(key_list[5], (ZF, NXF, NYF), jnp.float32) ** steps_of(key_list[5], (ZF, NXF, NYF), ((0, 2), (1, 8), (2, 8)), -0.2, 0.2)), 0.7, 1.4)
    coarse_now = gaussian(key_list[6], (3, ZC, NXC, NYC), 1.0, 6.0, ((1, 2), (2, 8), (3, 8)), jnp.float32)
    coarse_prev = gaussian(key_list[7], (3, ZC, NXC, NYC), 1.0, 6.0, ((1, 2), (2, 8), (3, 8)), jnp.float32)
    coarse_mu = jnp.clip(1.5 + 2.5 * jax.random.uniform(key_list[8], (ZC, NXC, NYC), jnp.float32) ** steps_of(key_list[8], (ZC, NXC, NYC), ((0, 2), (1, 8), (2, 8)), -0.2, 0.2), 1.5, 4.0)
    coarse_lam = jnp.clip(1.0 + 3.0 * jax.random.uniform(key_list[9], (ZC, NXC, NYC), jnp.float32) ** steps_of(key_list[9], (ZC, NXC, NYC), ((0, 2), (1, 8), (2, 8)), -0.2, 0.2), 1.0, 4.0)
    coarse_rho = jnp.clip(1.0 + 1.0 * jax.random.uniform(key_list[10], (ZC, NXC, NYC), jnp.float32) ** steps_of(key_list[10], (ZC, NXC, NYC), ((0, 2), (1, 8), (2, 8)), -0.2, 0.2), 1.0, 2.0)
    fine_ghost = gaussian(key_list[11], (3, NXF, NYF), 1.0, 6.0, ((1, 8), (2, 8)), jnp.float32)
    coarse_ghost = gaussian(key_list[12], (3, NXC, NYC), 1.0, 6.0, ((1, 8), (2, 8)), jnp.float32)
    return {"fine_now": fine_now, "fine_prev": fine_prev, "fine_mu": fine_mu, "fine_lam": fine_lam, "fine_rho": fine_rho, "fine_stretch": fine_stretch, "coarse_now": coarse_now, "coarse_prev": coarse_prev, "coarse_mu": coarse_mu, "coarse_lam": coarse_lam, "coarse_rho": coarse_rho, "fine_ghost": fine_ghost, "coarse_ghost": coarse_ghost}


step_squared = 0.09
first_weights = ((-2, 1.0 / 12.0), (-1, -8.0 / 12.0), (1, 8.0 / 12.0), (2, -1.0 / 12.0))
second_weights = ((-2, -1.0 / 12.0), (-1, 16.0 / 12.0), (0, -30.0 / 12.0), (1, 16.0 / 12.0), (2, -1.0 / 12.0))


def window(padded, offsets):
    height = padded.shape[0] - 4
    breadth = padded.shape[1] - 4
    length = padded.shape[2] - 4
    return padded[2 + offsets[0]:2 + offsets[0] + height, 2 + offsets[1]:2 + offsets[1] + breadth, 2 + offsets[2]:2 + offsets[2] + length]


def second(padded, dimension):
    summed = 0.0
    for offset, weight in second_weights:
        shift_vector = [0, 0, 0]
        shift_vector[dimension] = offset
        summed = summed + weight * window(padded, shift_vector)
    return summed


def cross_term(padded, dim_first, dim_second):
    summed = 0.0
    for offset_first, weight_first in first_weights:
        for offset_second, weight_second in first_weights:
            shift_vector = [0, 0, 0]
            shift_vector[dim_first] = offset_first
            shift_vector[dim_second] = offset_second
            summed = summed + (weight_first * weight_second) * window(padded, shift_vector)
    return summed


def operate(padded, shear, lame_lambda, stretch, inv_spacing):
    directions = (1, 2, 0)
    results = []
    for i in range(3):
        component = padded[i]
        vertical = second(component, 0)
        if stretch is not None:
            vertical = stretch * stretch * vertical
        laplace = second(component, 1) + second(component, 2) + vertical
        grad_div = jnp.zeros_like(laplace)
        for j in range(3):
            if i == j:
                contrib = second(padded[j], directions[i])
            else:
                contrib = cross_term(padded[j], directions[i], directions[j])
            if stretch is not None:
                if i == 2:
                    contrib = stretch * contrib
                if j == 2:
                    contrib = stretch * contrib
            grad_div = grad_div + contrib
        results.append((shear * laplace + (shear + lame_lambda) * grad_div) * inv_spacing)
    return jnp.stack(results)


def prolong(padded):
    extent = padded.shape[1] - 4
    coincide = padded[:, 2:extent + 2]
    between = (-padded[:, 1:extent + 1] + 9.0 * padded[:, 2:extent + 2] + 9.0 * padded[:, 3:extent + 3] - padded[:, 4:extent + 4]) / 16.0
    rows_done = jnp.stack([coincide, between], axis=2).reshape(padded.shape[0], 2 * extent, padded.shape[2])
    width_in = padded.shape[2] - 4
    coincide = rows_done[:, :, 2:width_in + 2]
    between = (-rows_done[:, :, 1:width_in + 1] + 9.0 * rows_done[:, :, 2:width_in + 2] + 9.0 * rows_done[:, :, 3:width_in + 3] - rows_done[:, :, 4:width_in + 4]) / 16.0
    return jnp.stack([coincide, between], axis=3).reshape(padded.shape[0], 2 * extent, 2 * width_in)


def restrict(padded):
    extent = (padded.shape[1] - 2) // 2
    rows_done = 0.25 * padded[:, 0:2 * extent:2] + 0.5 * padded[:, 1:2 * extent + 1:2] + 0.25 * padded[:, 2:2 * extent + 2:2]
    width_in = (padded.shape[2] - 2) // 2
    return 0.25 * rows_done[:, :, 0:2 * width_in:2] + 0.5 * rows_done[:, :, 1:2 * width_in + 1:2] + 0.25 * rows_done[:, :, 2:2 * width_in + 2:2]


def advance(current, previous, shear, lame_lambda, density, stretch, inv_spacing):
    margins = ((0, 0), (2, 2), (2, 2), (2, 2))
    acceleration = operate(jnp.pad(current, margins), shear, lame_lambda, stretch, inv_spacing) / density
    second_pass = operate(jnp.pad(acceleration, margins), shear, lame_lambda, stretch, inv_spacing) / density
    return 2.0 * current - previous + step_squared * acceleration + (step_squared * step_squared / 12.0) * second_pass


def reference(fine_now, fine_prev, fine_mu, fine_lam, fine_rho, fine_stretch, coarse_now, coarse_prev, coarse_mu, coarse_lam, coarse_rho, fine_ghost, coarse_ghost):
    fine_step = advance(fine_now, fine_prev, fine_mu, fine_lam, fine_rho, fine_stretch, 1.0)
    coarse_step = advance(coarse_now, coarse_prev, coarse_mu, coarse_lam, coarse_rho, None, 0.25)
    plane_fine = fine_step[:, -1]
    above_fine = fine_step[:, -2]
    plane_coarse = coarse_step[:, 0]
    below_coarse = coarse_step[:, 1]
    stiff_fine = fine_mu[-1] * fine_stretch[-1]
    stiff_coarse = coarse_mu[0]
    ghost_fine = fine_ghost
    ghost_coarse = coarse_ghost
    for iteration in range(SWEEPS):
        new_fine = prolong(jnp.pad(plane_coarse + ghost_coarse, ((0, 0), (2, 2), (2, 2)))) - plane_fine
        new_coarse = below_coarse - 2.0 * restrict(jnp.pad(stiff_fine * (ghost_fine - above_fine), ((0, 0), (1, 1), (1, 1)))) / stiff_coarse
        ghost_fine = new_fine
        ghost_coarse = new_coarse
    fine_next = jnp.concatenate([fine_step[:, :-1], (plane_fine + ghost_fine)[:, None]], axis=1)
    coarse_next = jnp.concatenate([(plane_coarse + ghost_coarse)[:, None], coarse_step[:, 1:]], axis=1)
    return fine_next, coarse_next
```

```python
import functools

import jax
import jax.numpy as jnp
import numpy as np
from jax import lax
from jax.experimental import pallas as pl
from jax.experimental.pallas import tpu as pltpu
from jax.sharding import PartitionSpec as P

DT2 = 0.09
DT4 = 0.09 * 0.09 / 12.0
LANES = 128
HIGHEST = lax.Precision.HIGHEST


def derivative_matrix():
    w = np.zeros((256, 256), np.float32)
    first = {-2: 1.0, -1: -8.0, 1: 8.0, 2: -1.0}
    second = {-2: -1.0, -1: 16.0, 0: -30.0, 1: 16.0, 2: -1.0}
    for lane in range(LANES):
        for base, weights in ((0, first), (LANES, second)):
            for offset, weight in weights.items():
                source = lane + offset
                row = source if 0 <= source < LANES else LANES + source % LANES
                w[row, base + lane] += weight
    return w


def diff1(f):
    return 8.0 * (f(1) - f(-1)) - (f(2) - f(-2))


def diff2(f, centre30):
    return 16.0 * (f(1) + f(-1)) - (f(2) + f(-2)) - centre30


def wave_kernel(
    rows, tiles, stretched, edge_k, now_hbm, coef_hbm, prev_ref, prev4_ref, w_ref,
    step_ref, edge_ref, now, acc, coef, dy, dyy, bb, ee, sem,
):
    g = lax.axis_index("grid")
    ext = rows + 16
    copies = []
    for t in range(tiles + 1):
        lanes = pl.ds(t * LANES, LANES)
        copies.append(pltpu.make_async_copy(now_hbm.at[:, :, :, lanes], now.at[:, pl.ds(2, 12), t], sem.at[0, t]))
        copies.append(pltpu.make_async_copy(coef_hbm.at[:, :, :, lanes], coef.at[:, :, t], sem.at[1, t]))
    for copy in copies:
        copy.start()
    for field in (now, acc):
        for z in (0, 1, 14, 15):
            field[:, z] = jnp.zeros((3, tiles + 1, ext, LANES), jnp.float32)
    for z in (0, 1, 14, 15):
        dy[:, z] = jnp.zeros((3, ext, LANES), jnp.float32)
        ee[z] = jnp.zeros((ext, LANES), jnp.float32)
    for copy in copies:
        copy.wait()

    low_half = lax.broadcasted_iota(jnp.int32, (ext, LANES), 1) < 64

    def y_stage(src, t, z):
        after = jnp.where(t == tiles, 0, t + 1)
        before = jnp.where(t == 0, tiles, t - 1)
        parts = []
        for c in range(3):
            side = jnp.where(low_half, src[c, z + 2, after], src[c, z + 2, before])
            parts.append(jnp.concatenate([src[c, z + 2, t], side], axis=1))
        whole = jnp.concatenate(parts, axis=0)
        high = whole.astype(jnp.bfloat16)
        low = (whole - high.astype(jnp.float32)).astype(jnp.bfloat16)
        out = jnp.dot(high, w_ref[...], preferred_element_type=jnp.float32)
        out = out + jnp.dot(low, w_ref[...], preferred_element_type=jnp.float32)
        for c in range(3):
            dy[c, z + 2] = out[c * ext : (c + 1) * ext, :LANES]
            dyy[c, z] = out[c * ext : (c + 1) * ext, LANES:]

    def mid_stage(src, t, z):
        for r in range(0, ext, 8):
            at = pl.ds(r, 8)
            bb[z, at, :] = diff1(lambda o: src[2, z + 2 + o, t, at, :])
        for r in range(6, ext - 2, 8):
            along = diff1(lambda o: src[0, z + 2, t, pl.ds(r + o, 8), :])
            ee[z + 2, pl.ds(r, 8), :] = along + dy[1, z + 2, pl.ds(r, 8), :]

    def operator(src, t, z, r):
        at = pl.ds(r, 8)
        c1 = coef[0, z, t, at, :]
        c2 = coef[1, z, t, at, :]
        twelfth = 1.0 / 12.0
        laps, xx, zz = [], [], []
        for c in range(3):
            c30 = 30.0 * src[c, z + 2, t, at, :]
            xx.append(diff2(lambda o: src[c, z + 2, t, pl.ds(r + o, 8), :], c30))
            zz.append(diff2(lambda o: src[c, z + 2 + o, t, at, :], c30))
        yy = [dyy[c, z, at, :] for c in range(3)]
        xy_y = diff1(lambda o: dy[1, z + 2, pl.ds(r + o, 8), :])
        xz_z = diff1(lambda o: bb[z, pl.ds(r + o, 8), :])
        xy_x = diff1(lambda o: dy[0, z + 2, pl.ds(r + o, 8), :])
        yz_z = diff1(lambda o: dy[2, z + 2 + o, at, :])
        z_of = diff1(lambda o: ee[z + 2 + o, at, :])
        if stretched:
            s = coef[2, z, t, at, :]
            s2 = s * s
            zz = [s2 * v for v in zz]
            xz_z, yz_z, z_of = s * xz_z, s * yz_z, s * z_of
        laps = [xx[c] + yy[c] + zz[c] for c in range(3)]
        return (
            c1 * laps[0] + c2 * (xx[0] + twelfth * (xy_y + xz_z)),
            c1 * laps[1] + c2 * (yy[1] + twelfth * (xy_x + yz_z)),
            c1 * laps[2] + c2 * (zz[2] + twelfth * z_of),
        )

    def loop(n, f):
        lax.fori_loop(0, n, lambda i, carry: (f(i), carry)[1], 0)

    def first_pass(t):
        loop(12, lambda z: y_stage(now, t, z))
        loop(12, lambda z: mid_stage(now, t, z))

        def layer(i):
            z = i + 2 * g
            for r in range(6, ext - 2, 8):
                for c, value in enumerate(operator(now, t, z, r)):
                    acc[c, z + 2, t, pl.ds(r, 8), :] = value

        loop(10, layer)

    loop(tiles + 1, first_pass)

    def finish(t, z, r, previous, store):
        at = pl.ds(r, 8)
        for c, value in enumerate(operator(acc, t, z, r)):
            total = 2.0 * now[c, z + 2, t, at, :] - previous(c) + DT2 * acc[c, z + 2, t, at, :] + DT4 * value
            store(c, total)

    for t in range(tiles + 1):
        loop(10, lambda i: y_stage(acc, t, i + 2 * g))
        loop(10, lambda i: mid_stage(acc, t, i + 2 * g))
        if t < tiles:
            lanes = pl.ds(t * LANES, LANES)

            def layer(k):
                z = k + 4 * g
                for r in range(8, rows + 8, 8):
                    at = pl.ds(r - 8, 8)

                    def store(c, value):
                        step_ref[c, k, at, lanes] = value

                    finish(t, z, r, lambda c: prev_ref[c, k, at, lanes], store)

            loop(8, layer)
        else:

            def layer(i):
                z = edge_k + i + 4 * g
                for r in range(8, rows + 8, 8):
                    at = pl.ds(r - 8, 8)

                    def store(c, value):
                        edge_ref[c, i, at, :] = value

                    finish(t, z, r, lambda c: prev4_ref[c, i, at, :], store)

            loop(2, layer)


def wave(now_x, coef_x, prev, prev4, stretched, edge_k):
    rows, cols = prev.shape[2:]
    tiles = cols // LANES
    ext = rows + 16
    vmem = pl.BlockSpec(memory_space=pltpu.VMEM)
    hbm = pl.BlockSpec(memory_space=pl.ANY)
    f32 = jnp.float32
    units = 3 * (10 * (ext - 8) // 8 * (tiles + 1) + rows * tiles)
    return pl.pallas_call(
        functools.partial(wave_kernel, rows, tiles, stretched, edge_k),
        out_shape=(
            jax.ShapeDtypeStruct((3, 8, rows, cols), f32),
            jax.ShapeDtypeStruct((3, 2, rows, LANES), f32),
        ),
        in_specs=[hbm, hbm, vmem, vmem, vmem],
        out_specs=(vmem, vmem),
        scratch_shapes=[
            pltpu.VMEM((3, 16, tiles + 1, ext, LANES), f32),
            pltpu.VMEM((3, 16, tiles + 1, ext, LANES), f32),
            pltpu.VMEM((coef_x.shape[0], 12, tiles + 1, ext, LANES), f32),
            pltpu.VMEM((3, 16, ext, LANES), f32),
            pltpu.VMEM((3, 12, ext, LANES), f32),
            pltpu.VMEM((12, ext, LANES), f32),
            pltpu.VMEM((16, ext, LANES), f32),
            pltpu.SemaphoreType.DMA((2, tiles + 1)),
        ],
        compiler_params=pltpu.CompilerParams(vmem_limit_bytes=56 * 2**20),
        cost_estimate=pl.CostEstimate(flops=units * 100000, bytes_accessed=10 * 2**20, transcendentals=0),
    )(now_x, coef_x, prev, prev4, jnp.asarray(derivative_matrix(), jnp.bfloat16))


def ring(value, axis, by):
    n = lax.axis_size(axis)
    return lax.ppermute(value, axis, [(i, (i + by) % n) for i in range(n)])


def swap(value):
    return lax.ppermute(value, "grid", [(0, 1), (1, 0)])


def neighbours(pieces, axis):
    n = lax.axis_size(axis)
    index = lax.axis_index(axis)
    lows = [lax.slice_in_dim(a, a.shape[d] - lo, a.shape[d], axis=d) for a, d, lo, up in pieces]
    ups = [lax.slice_in_dim(a, 0, up, axis=d) for a, d, lo, up in pieces]

    def move(parts, by, keep):
        flat = jnp.concatenate([p.reshape(-1) for p in parts])
        flat = jnp.pad(flat, (0, -flat.size % 1024)).reshape(-1, LANES)
        flat = jnp.where(keep, ring(flat, axis, by), 0.0).reshape(-1)
        out, at = [], 0
        for p in parts:
            out.append(lax.slice_in_dim(flat, at, at + p.size).reshape(p.shape))
            at += p.size
        return out

    return list(zip(move(lows, 1, index > 0), move(ups, -1, index < n - 1)))


def lane_tile(low, up):
    gap = jnp.zeros(low.shape[:-1] + (LANES - low.shape[-1] - up.shape[-1],), jnp.float32)
    return jnp.concatenate([up, gap, low], axis=-1)


def prolong_matrix(m_rows, m_at, x_rows, x_at):
    out = np.zeros((x_rows, m_rows), np.float32)
    where = {m_at(j): j for j in range(m_rows)}
    for i in range(x_rows):
        x = x_at(i)
        m = x // 2
        weights = {m: 1.0} if x % 2 == 0 else {m - 1: -1 / 16, m: 9 / 16, m + 1: 9 / 16, m + 2: -1 / 16}
        for target, weight in weights.items():
            if target in where:
                out[i, where[target]] = weight
    return out


def restrict_matrix(m_rows, m_at, x_rows, x_at):
    out = np.zeros((m_rows, x_rows), np.float32)
    where = {x_at(i): i for i in range(x_rows)}
    for j in range(m_rows):
        m = m_at(j)
        for target, weight in {2 * m - 1: 0.25, 2 * m: 0.5, 2 * m + 1: 0.25}.items():
            if target in where:
                out[j, where[target]] = weight
    return out


def body(
    fine_now, fine_prev, fine_mu, fine_lam, fine_rho, fine_stretch,
    coarse_now, coarse_prev, coarse_mu, coarse_lam, coarse_rho, fine_ghost, coarse_ghost,
):
    g = lax.axis_index("grid")
    upper = g == 0
    fine_coef = jnp.stack([fine_mu / (12.0 * fine_rho), (fine_mu + fine_lam) / (12.0 * fine_rho), fine_stretch])
    coarse_coef = jnp.stack([coarse_mu / (48.0 * coarse_rho), (coarse_mu + coarse_lam) / (48.0 * coarse_rho)])
    stiff = fine_mu[7] * fine_stretch[7]
    flex = 2.0 / coarse_mu[0]
    y = neighbours(
        [
            (fine_now, 3, 9, 8), (fine_coef, 3, 7, 6), (fine_prev[:, 6:8], 3, 5, 4), (fine_ghost, 2, 5, 4), (stiff, 1, 5, 4),
            (coarse_now, 3, 7, 8), (coarse_coef, 3, 5, 6), (coarse_prev[:, 0:2], 3, 3, 4), (coarse_ghost, 2, 3, 4), (flex, 1, 3, 4),
        ],
        "gy",
    )
    y = [lane_tile(low, up) for low, up in y]
    wide = lambda a, b: jnp.concatenate([a, b], axis=-1)
    blocks = [wide(fine_now, y[0]), wide(fine_coef, y[1]), wide(coarse_now, y[5]), wide(coarse_coef, y[6])]
    x = neighbours([(blocks[0], 2, 4, 4), (blocks[1], 2, 2, 2), (blocks[2], 2, 4, 4), (blocks[3], 2, 2, 2)], "gx")
    grown = []
    for block, (low, up) in zip(blocks, x):
        gap = lambda a: jnp.zeros(a.shape[:2] + (8 - a.shape[2], a.shape[3]), jnp.float32)
        grown.append(jnp.concatenate([gap(low), low, block, up, gap(up)], axis=2))
    windows = []
    for block in grown:
        other = swap(jnp.where(upper, block[:, 4:], block[:, :4]))
        windows.append(
            jnp.where(upper, jnp.concatenate([block, other], axis=1), jnp.concatenate([other, block], axis=1))
        )
    fine_step, fine_edge = wave(windows[0], windows[1], fine_prev, y[2], True, 6)
    coarse_step, coarse_edge = wave(windows[2], windows[3], coarse_prev, y[7], False, 0)

    plane_fine = wide(fine_step[:, 7], fine_edge[:, 1])
    above_fine = wide(fine_step[:, 6], fine_edge[:, 0])
    plane_coarse = wide(coarse_step[:, 0], coarse_edge[:, 0])
    below_coarse = wide(coarse_step[:, 1], coarse_edge[:, 1])
    stiff = wide(stiff, y[4])
    flex = wide(flex, y[9])
    fine_planes = jnp.concatenate(
        [plane_fine + above_fine, stiff * (wide(fine_ghost, y[3]) - above_fine), stiff[None]]
    )
    coarse_planes = jnp.concatenate(
        [plane_coarse + below_coarse, plane_coarse + wide(coarse_ghost, y[8]), flex[None]]
    )
    (fl, fu), (cl, cu) = neighbours([(fine_planes, 1, 5, 4), (coarse_planes, 1, 3, 4)], "gx")
    pad = lambda a, n, side: jnp.pad(a, ((0, 0), (n, 0) if side else (0, n), (0, 0)))
    fine_planes = jnp.concatenate([pad(fl, 3, 1), fine_planes, pad(fu, 4, 0)], axis=1)
    coarse_planes = jnp.concatenate([pad(cl, 1, 1), coarse_planes, cu], axis=1)
    fine_other, coarse_other = swap(fine_planes), swap(coarse_planes)
    fine_planes = jnp.where(upper, fine_other, fine_planes)
    coarse_planes = jnp.where(upper, coarse_planes, coarse_other)

    fine_rows, fine_cols = fine_planes.shape[1:]
    coarse_rows, coarse_cols = coarse_planes.shape[1:]
    at_rows = (lambda i: i - 4, lambda i: i - 8)
    cyclic = lambda n: lambda i: i if i < n - LANES // 2 else i - n
    at_cols = (cyclic(coarse_cols), cyclic(fine_cols))
    px = prolong_matrix(coarse_rows, at_rows[0], fine_rows, at_rows[1])
    py = prolong_matrix(coarse_cols, at_cols[0], fine_cols, at_cols[1])
    rx = restrict_matrix(coarse_rows, at_rows[0], fine_rows, at_rows[1])
    ry = restrict_matrix(coarse_cols, at_cols[0], fine_cols, at_cols[1])
    both = lambda mx, my, v: jnp.einsum(
        "ax,nxb->nab", mx, jnp.einsum("nxy,by->nxb", v, my, precision=HIGHEST), precision=HIGHEST
    )
    u, w, s = fine_planes[:3], fine_planes[3:6], fine_planes[6]
    p, q, f = coarse_planes[:3], coarse_planes[3:6], coarse_planes[6]
    start = jnp.where(upper, p - both(rx, ry, w) * f, q)
    end = p - both(rx, ry, s * (both(px, py, start) - u)) * f
    fine_plane = both(px, py, end)[:, 8:-8, :512]
    coarse_plane = end[:, 4:-4, :256]
    fine_out = jnp.where(upper, fine_step[:, 7], fine_plane)
    coarse_out = jnp.where(upper, coarse_plane, coarse_step[:, 0])
    fine_next = jnp.concatenate([fine_step[:, :7], fine_out[:, None]], axis=1)
    coarse_next = jnp.concatenate([coarse_out[:, None], coarse_step[:, 1:]], axis=1)
    return fine_next, coarse_next


def solution(mesh):
    block = P(None, "grid", "gx", "gy")
    scalar = P("grid", "gx", "gy")
    plane = P(None, "gx", "gy")
    return jax.shard_map(
        body,
        mesh=mesh,
        in_specs=(block, block, scalar, scalar, scalar, scalar, block, block, scalar, scalar, scalar, plane, plane),
        out_specs=(block, block),
        check_vma=False,
    )
```

```python
import functools

import jax
import jax.numpy as jnp
import numpy as np
from jax import lax
from jax.experimental import pallas as pl
from jax.experimental.pallas import tpu as pltpu
from jax.sharding import PartitionSpec as P

DT2 = 0.09
DT4 = 0.09 * 0.09 / 12.0
LANES = 128
C1, C2 = 4, 5
HIGHEST = lax.Precision.HIGHEST


def derivative_matrix():
    w = np.zeros((256, 256), np.float32)
    first = {-2: 1.0, -1: -8.0, 1: 8.0, 2: -1.0}
    second = {-2: -1.0, -1: 16.0, 0: -30.0, 1: 16.0, 2: -1.0}
    for lane in range(LANES):
        for base, weights in ((0, first), (LANES, second)):
            for offset, weight in weights.items():
                source = lane + offset
                row = source if 0 <= source < LANES else LANES + source % LANES
                w[row, base + lane] += weight
    return w


def diff1(f):
    return 8.0 * (f(1) - f(-1)) - (f(2) - f(-2))


def diff2(f, centre30):
    return 16.0 * (f(1) + f(-1)) - (f(2) + f(-2)) - centre30


def near_base(g):
    return 4 * (1 - g)


def wave_kernel(
    rows, tiles, stretched, edge_k, block0, block_z, *refs,
):
    (now_hbm, coef_hbm, stretch_hbm, znow_hbm, zcoef_hbm, side_hbm, zside_hbm,
     low_ref, up_ref, zlow_ref, zup_ref, prev_ref, prev4_ref, w_ref,
     step_ref, edge_ref, now, acc, coef, dy, dyy, bb, ee, lhs, sem) = refs
    g = lax.axis_index("grid")
    gx = lax.axis_index("gx")
    ext = rows + 16
    n_coef = 3 if stretched else 2
    own, own_c = 2 + 4 * g, 4 * g
    zed, zed_c = 10 - 8 * g, 8 - 6 * g
    core = pl.ds(8, rows)
    copies = []

    def fetch(src, dst):
        copies.append(pltpu.make_async_copy(src, dst, sem.at[len(copies)]))

    for t in range(tiles):
        lanes = pl.ds(t * LANES, LANES)
        fetch(now_hbm.at[:, :, :, lanes], now.at[:, pl.ds(own, 8), t, core])
        fetch(coef_hbm.at[:, :, :, lanes], coef.at[pl.ds(0, 2), pl.ds(own_c, 8), t, core])
        fetch(znow_hbm.at[:, :, :, lanes], now.at[:, pl.ds(zed, 4), t, core])
        fetch(zcoef_hbm.at[:, :, :, lanes], coef.at[:, pl.ds(zed_c, 2), t, core])
        if stretched:
            fetch(stretch_hbm.at[:, :, lanes], coef.at[2, pl.ds(own_c, 8), t, core])
    fetch(side_hbm.at[pl.ds(0, 3)], now.at[:, pl.ds(own, 8), tiles, core])
    fetch(side_hbm.at[pl.ds(3, n_coef)], coef.at[:, pl.ds(own_c, 8), tiles, core])
    fetch(zside_hbm.at[pl.ds(0, 3)], now.at[:, pl.ds(zed, 4), tiles, core])
    fetch(zside_hbm.at[pl.ds(3, n_coef)], coef.at[:, pl.ds(8 - 8 * g, 4), tiles, core])
    for copy in copies:
        copy.start()
    for field in (now, acc):
        for z in (0, 1, 14, 15):
            field[:, z] = jnp.zeros((3, tiles + 1, ext, LANES), jnp.float32)
    for z in (0, 1, 14, 15):
        dy[:, z] = jnp.zeros((3, ext, LANES), jnp.float32)
        ee[z] = jnp.zeros((ext, LANES), jnp.float32)
    near = near_base(g)
    n_now, width = 6 * (tiles + 1), tiles + 1
    last = lax.axis_size("gx") - 1
    for ref, keep, at_now, at_coef in ((low_ref, gx > 0, 4, 6), (up_ref, gx < last, rows + 8, rows + 8)):
        zref = zlow_ref if ref is low_ref else zup_ref
        groups = ((ref, block0, near), (ref, block0 + block_z, 4 - near), (zref, block0, 8 - 12 * g + 4 * g))
        for source, base, layer in groups:
            first = layer if source is zref else layer + 4 * g
            for t in range(width):
                for c in range(3):
                    for i in range(2):
                        v = jnp.where(keep, source[base + (c * 2 + i) * width + t], 0.0)
                        for h in range(2):
                            now[c, first + 2 + 2 * i + h, t, pl.ds(at_now, 4), :] = v[4 * h : 4 * h + 4]
                for c in range(n_coef):
                    v = jnp.where(keep, source[base + n_now + c * width + t], 0.0)
                    for h in range(4):
                        coef[c, first + h, t, pl.ds(at_coef, 2), :] = v[2 * h : 2 * h + 2]
    for copy in copies:
        copy.wait()

    low_half = lax.broadcasted_iota(jnp.int32, (ext, LANES), 1) < 64

    def y_stage(src, t, z0, chunk):
        after = jnp.where(t == tiles, 0, t + 1)
        before = jnp.where(t == 0, tiles, t - 1)
        n = chunk * 3 * ext
        for k in range(chunk):
            for c in range(3):
                z = z0 + k
                at = pl.ds((k * 3 + c) * ext, ext)
                at_low = pl.ds(n + (k * 3 + c) * ext, ext)
                side = jnp.where(low_half, src[c, z + 2, after], src[c, z + 2, before])
                for h, v in enumerate((src[c, z + 2, t], side)):
                    high = v.astype(jnp.bfloat16)
                    lanes = pl.ds(h * LANES, LANES)
                    lhs[at, lanes] = high
                    lhs[at_low, lanes] = (v - high.astype(jnp.float32)).astype(jnp.bfloat16)
        out = jnp.dot(lhs[pl.ds(0, 2 * n), :], w_ref[...], preferred_element_type=jnp.float32)
        out = out[:n] + out[n:]
        for k in range(chunk):
            for c in range(3):
                r0 = (k * 3 + c) * ext
                dy[c, z0 + k + 2] = out[r0 : r0 + ext, :LANES]
                dyy[c, z0 + k] = out[r0 : r0 + ext, LANES:]

    def mid_stage(src, t, z):
        for r in range(0, ext, 8):
            at = pl.ds(r, 8)
            bb[z, at, :] = diff1(lambda o: src[2, z + 2 + o, t, at, :])
        for r in range(6, ext - 2, 8):
            along = diff1(lambda o: src[0, z + 2, t, pl.ds(r + o, 8), :])
            ee[z + 2, pl.ds(r, 8), :] = along + dy[1, z + 2, pl.ds(r, 8), :]

    def operator(src, t, z, r):
        at = pl.ds(r, 8)
        c1 = coef[0, z, t, at, :]
        c2 = coef[1, z, t, at, :]
        twelfth = 1.0 / 12.0
        laps, xx, zz = [], [], []
        for c in range(3):
            c30 = 30.0 * src[c, z + 2, t, at, :]
            xx.append(diff2(lambda o: src[c, z + 2, t, pl.ds(r + o, 8), :], c30))
            zz.append(diff2(lambda o: src[c, z + 2 + o, t, at, :], c30))
        yy = [dyy[c, z, at, :] for c in range(3)]
        xy_y = diff1(lambda o: dy[1, z + 2, pl.ds(r + o, 8), :])
        xz_z = diff1(lambda o: bb[z, pl.ds(r + o, 8), :])
        xy_x = diff1(lambda o: dy[0, z + 2, pl.ds(r + o, 8), :])
        yz_z = diff1(lambda o: dy[2, z + 2 + o, at, :])
        z_of = diff1(lambda o: ee[z + 2 + o, at, :])
        if stretched:
            s = coef[2, z, t, at, :]
            s2 = s * s
            zz = [s2 * v for v in zz]
            xz_z, yz_z, z_of = s * xz_z, s * yz_z, s * z_of
        laps = [xx[c] + yy[c] + zz[c] for c in range(3)]
        return (
            c1 * laps[0] + c2 * (xx[0] + twelfth * (xy_y + xz_z)),
            c1 * laps[1] + c2 * (yy[1] + twelfth * (xy_x + yz_z)),
            c1 * laps[2] + c2 * (zz[2] + twelfth * z_of),
        )

    def loop(n, f):
        lax.fori_loop(0, n, lambda i, carry: (f(i), carry)[1], 0)

    def first_pass(t):
        loop(12 // C1, lambda i: y_stage(now, t, C1 * i, C1))
        loop(12, lambda z: mid_stage(now, t, z))

        def layer(i):
            z = i + 2 * g
            for r in range(6, ext - 2, 8):
                for c, value in enumerate(operator(now, t, z, r)):
                    acc[c, z + 2, t, pl.ds(r, 8), :] = value

        loop(10, layer)

    loop(tiles + 1, first_pass)

    def finish(t, z, r, previous, store):
        at = pl.ds(r, 8)
        for c, value in enumerate(operator(acc, t, z, r)):
            total = 2.0 * now[c, z + 2, t, at, :] - previous(c) + DT2 * acc[c, z + 2, t, at, :] + DT4 * value
            store(c, total)

    for t in range(tiles + 1):
        loop(10 // C2, lambda i: y_stage(acc, t, C2 * i + 2 * g, C2))
        loop(10, lambda i: mid_stage(acc, t, i + 2 * g))
        if t < tiles:
            lanes = pl.ds(t * LANES, LANES)

            def layer(k):
                z = k + 4 * g
                for r in range(8, rows + 8, 8):
                    at = pl.ds(r - 8, 8)

                    def store(c, value):
                        step_ref[c, k, at, lanes] = value

                    finish(t, z, r, lambda c: prev_ref[c, k, at, lanes], store)

            loop(8, layer)
        else:

            def layer(i):
                z = edge_k + i + 4 * g
                for r in range(8, rows + 8, 8):
                    at = pl.ds(r - 8, 8)

                    def store(c, value):
                        edge_ref[c, i, at, :] = value

                    finish(t, z, r, lambda c: prev4_ref[c, i, at, :], store)

            loop(2, layer)


def wave(now, coef, stretch, znow, zcoef, side, zside, low, up, zlow, zup, prev, prev4, edge_k, block0, block_z):
    rows, cols = prev.shape[2:]
    tiles = cols // LANES
    ext = rows + 16
    stretched = zcoef.shape[0] == 3
    vmem = pl.BlockSpec(memory_space=pltpu.VMEM)
    hbm = pl.BlockSpec(memory_space=pl.ANY)
    f32 = jnp.float32
    units = 3 * (10 * (ext - 8) // 8 * (tiles + 1) + rows * tiles)
    return pl.pallas_call(
        functools.partial(wave_kernel, rows, tiles, stretched, edge_k, block0, block_z),
        out_shape=(
            jax.ShapeDtypeStruct((3, 8, rows, cols), f32),
            jax.ShapeDtypeStruct((3, 2, rows, LANES), f32),
        ),
        in_specs=[hbm] * 7 + [vmem] * 7,
        out_specs=(vmem, vmem),
        scratch_shapes=[
            pltpu.VMEM((3, 16, tiles + 1, ext, LANES), f32),
            pltpu.VMEM((3, 16, tiles + 1, ext, LANES), f32),
            pltpu.VMEM((zcoef.shape[0], 12, tiles + 1, ext, LANES), f32),
            pltpu.VMEM((3, 16, ext, LANES), f32),
            pltpu.VMEM((3, 12, ext, LANES), f32),
            pltpu.VMEM((12, ext, LANES), f32),
            pltpu.VMEM((16, ext, LANES), f32),
            pltpu.VMEM((max(C1, C2) * 6 * ext, 256), jnp.bfloat16),
            pltpu.SemaphoreType.DMA((5 * tiles + 4,)),
        ],
        compiler_params=pltpu.CompilerParams(vmem_limit_bytes=56 * 2**20),
        cost_estimate=pl.CostEstimate(flops=units * 100000, bytes_accessed=10 * 2**20, transcendentals=0),
    )(now, coef, stretch, znow, zcoef, side, zside, low, up, zlow, zup, prev, prev4, jnp.asarray(derivative_matrix(), jnp.bfloat16))


def slots(widths):
    out, tile, lane = [], 0, 0
    for width in widths:
        if lane + width > LANES:
            tile, lane = tile + 1, 0
        out.append((tile, lane))
        lane += width
    return out, tile + 1


FINE_HALO = ((9, 8), (7, 6), (5, 4), (5, 4), (5, 4))
COARSE_HALO = ((7, 8), (5, 6), (3, 4), (3, 4), (3, 4))


def items_of(halo, n_coef):
    kinds = [0] * 24 + [1] * (8 * n_coef) + [2] * 6 + [3] * 3 + [4]
    halos = [halo[k] for k in kinds]
    places, n_tiles = slots([max(h) for h in halos])
    return halos, places, n_tiles


def lane_between(lane, first, width):
    first = first % LANES
    if first + width <= LANES:
        return (lane >= first) & (lane < first + width)
    return (lane >= first) | (lane < first + width - LANES)


def pack_kernel(*refs):
    fine_in, coarse_in, (low_ref, up_ref) = refs[:14], refs[14:26], refs[26:]
    block = 0
    for rows, ins, halo, n_coef in ((64, fine_in, FINE_HALO, 3), (32, coarse_in, COARSE_HALO, 2)):
        halos, places, n_tiles = items_of(halo, n_coef)
        lane = lax.broadcasted_iota(jnp.int32, (rows, LANES), 1)
        half = lane < 64
        pick = lambda i, *at: jnp.where(half, ins[2 * i][at], ins[2 * i + 1][at])
        scale = 12.0 if n_coef == 3 else 48.0

        def coefficients(z):
            mu, lam = pick(1, z), pick(2, z)
            inverse = 1.0 / (scale * pick(3, z))
            out = [mu * inverse, (mu + lam) * inverse]
            return out + [pick(4, z)] if n_coef == 3 else out

        values = [lambda c=c, z=z: pick(0, c, z) for c in range(3) for z in range(8)]
        held = {}

        def coefficient(c, z):
            if z not in held:
                held[z] = coefficients(z)
            return held[z][c]

        values += [lambda c=c, z=z: coefficient(c, z) for z in range(8) for c in range(n_coef)]
        at = 5 if n_coef == 3 else 4
        values += [lambda c=c, z=z: pick(at, c, z) for c in range(3) for z in range(2)]
        values += [lambda c=c: pick(at + 1, c) for c in range(3)]
        if n_coef == 3:
            values.append(lambda: pick(1, 7) * pick(4, 7))
        else:
            values.append(lambda: 2.0 / pick(1, 0))
        for tile in range(n_tiles):
            low = jnp.zeros((rows, LANES), jnp.float32)
            up = jnp.zeros((rows, LANES), jnp.float32)
            for value, (lo, hi), (home, first) in zip(values, halos, places):
                if home == tile:
                    turned = value()
                    turned = pltpu.roll(turned, first, 1) if first else turned
                    low = jnp.where(lane_between(lane, first, hi), turned, low)
                    up = jnp.where(lane_between(lane, first - lo, lo), turned, up)
            for r in range(rows // 8):
                low_ref[block] = low[8 * r : 8 * r + 8]
                up_ref[block] = up[8 * r : 8 * r + 8]
                block += 1


Y_BLOCKS = 8 * items_of(FINE_HALO, 3)[2] + 4 * items_of(COARSE_HALO, 2)[2]


def pack(fine, coarse):
    specs, operands = [], []
    for arrays, layer_of_prev, tiles in ((fine, 3, 4), (coarse, 0, 2)):
        for i, a in enumerate(arrays):
            block = list(a.shape[:-1]) + [LANES]
            at = [0] * a.ndim
            if i == len(arrays) - 2:
                block[1], at[1] = 2, layer_of_prev
            for tile in (0, tiles - 1):
                where = tuple(at[:-1] + [tile])
                specs.append(pl.BlockSpec(tuple(block), lambda i, where=where: where))
                operands.append(a)
    out = jax.ShapeDtypeStruct((Y_BLOCKS, 8, LANES), jnp.float32)
    whole = pl.BlockSpec((Y_BLOCKS, 8, LANES), lambda i: (0, 0, 0))
    return pl.pallas_call(
        pack_kernel, grid=(1,), out_shape=(out, out), in_specs=specs, out_specs=(whole, whole),
        compiler_params=pltpu.CompilerParams(vmem_limit_bytes=56 * 2**20),
    )(*operands)


def coefficient_kernel(scales, *refs):
    n = len(scales)
    for i, scale in enumerate(scales):
        mu, lam, rho = refs[3 * i : 3 * i + 3]
        out = refs[3 * n + i]

        def layer(z, carry, mu=mu, lam=lam, rho=rho, out=out, scale=scale):
            inverse = 1.0 / (scale * rho[z])
            out[0, z] = mu[z] * inverse
            out[1, z] = (mu[z] + lam[z]) * inverse
            return carry

        lax.fori_loop(0, 8, layer, 0)


def coefficients(fine, coarse):
    vmem = pl.BlockSpec(memory_space=pltpu.VMEM)
    outs = tuple(jax.ShapeDtypeStruct((2,) + a[0].shape, jnp.float32) for a in (fine, coarse))
    return pl.pallas_call(
        functools.partial(coefficient_kernel, (12.0, 48.0)), out_shape=outs, in_specs=[vmem] * 6, out_specs=(vmem, vmem),
        compiler_params=pltpu.CompilerParams(vmem_limit_bytes=56 * 2**20),
        cost_estimate=pl.CostEstimate(flops=10**7, bytes_accessed=7 * 2**20, transcendentals=0),
    )(*fine, *coarse)


def unpack_kernel(*refs):
    from_up, from_low = refs[:2]
    fine_edges, coarse_edges = refs[2:8], refs[8:12]
    fine_out, coarse_out, (low_ref, up_ref) = refs[12:16], refs[16:20], refs[20:]
    g = lax.axis_index("grid")
    gy = lax.axis_index("gy")
    keep_low, keep_up = gy > 0, gy < lax.axis_size("gy") - 1
    near = near_base(g)
    block0 = 0
    for rows, halo, n_coef, outs in ((64, FINE_HALO, 3, fine_out), (32, COARSE_HALO, 2, coarse_out)):
        halos, places, n_tiles = items_of(halo, n_coef)
        lane = lax.broadcasted_iota(jnp.int32, (rows, LANES), 1)
        side_ref, prev_ref, ghost_ref, stiff_ref = outs
        stores = [lambda v, c=c, z=z: side_ref.__setitem__((c, z), v) for c in range(3) for z in range(8)]
        stores += [lambda v, c=c, z=z: side_ref.__setitem__((3 + c, z), v) for z in range(8) for c in range(n_coef)]
        stores += [lambda v, c=c, z=z: prev_ref.__setitem__((c, z), v) for c in range(3) for z in range(2)]
        stores += [lambda v, c=c: ghost_ref.__setitem__((c,), v) for c in range(3)]
        stores += [lambda v: stiff_ref.__setitem__((Ellipsis,), v)]
        tiles = []
        for tile in range(n_tiles):
            at = pl.ds(block0 + tile * rows // 8, rows // 8)
            tiles.append((from_up[at].reshape(rows, LANES), from_low[at].reshape(rows, LANES)))
        block0 += n_tiles * rows // 8
        for store, (lo, hi), (home, first) in zip(stores, halos, places):
            up, low = tiles[home]
            both = jnp.where(lane_between(lane, first, hi), up, low)
            both = pltpu.roll(both, LANES - first, 1) if first else both
            valid = ((lane < hi) & keep_up) | ((lane >= LANES - lo) & keep_low)
            store(jnp.where(valid, both, 0.0))
    base, far_base = 0, X_NEAR
    for rows, width, n_coef, outs, edges in ((64, 5, 3, fine_out, fine_edges), (32, 3, 2, coarse_out, coarse_edges)):
        side_ref = outs[0]
        first_rows, last_rows = edges[0::2], edges[1::2]
        for msg, edge, is_last in ((low_ref, first_rows, False), (up_ref, last_rows, True)):
            for start, layer0 in ((base, near), (far_base, 4 - near)):
                for t in range(width):
                    lanes = pl.ds(t * LANES, LANES)

                    def rows_of(kind, c, z, count):
                        if t == width - 1:
                            tile = pl.ds(rows - 8, 8) if is_last else pl.ds(0, 8)
                            v = side_ref[3 * kind + c, z, tile, :]
                        elif kind == 0:
                            v = edge[0][c, z, :, lanes]
                        elif c < 2:
                            v = edge[1][c, z, :, lanes]
                        else:
                            v = edge[2][z, :, lanes]
                        return v[8 - count :] if is_last else v[:count]

                    for c in range(3):
                        for i in range(2):
                            parts = [rows_of(0, c, layer0 + 2 * i + h, 4) for h in range(2)]
                            msg[start + (c * 2 + i) * width + t] = jnp.concatenate(parts, axis=0)
                    for c in range(n_coef):
                        parts = [rows_of(1, c, layer0 + h, 2) for h in range(4)]
                        msg[start + (6 + c) * width + t] = jnp.concatenate(parts, axis=0)
        base += (6 + n_coef) * width
        far_base += (6 + n_coef) * width


X_FINE = 9 * 5
X_NEAR = 9 * 5 + 8 * 3


def unpack(from_up, from_low, fine, coarse):
    vmem = pl.BlockSpec(memory_space=pltpu.VMEM)
    specs, operands = [], []
    whole = pl.BlockSpec((Y_BLOCKS, 8, LANES), lambda i: (0, 0, 0))
    for arrays in (fine, coarse):
        for a in arrays:
            block = list(a.shape)
            block[-2] = 8
            for tile in (0, a.shape[-2] // 8 - 1):
                where = tuple([0] * (a.ndim - 2) + [tile, 0])
                specs.append(pl.BlockSpec(tuple(block), lambda i, where=where: where))
                operands.append(a)
    shapes = []
    for rows, n_coef in ((64, 3), (32, 2)):
        shapes += [(3 + n_coef, 8, rows, LANES), (3, 2, rows, LANES), (3, rows, LANES), (rows, LANES)]
    shapes += [(2 * X_NEAR, 8, LANES)] * 2
    return pl.pallas_call(
        unpack_kernel, grid=(1,),
        out_shape=tuple(jax.ShapeDtypeStruct(s, jnp.float32) for s in shapes),
        in_specs=[whole, whole] + specs,
        out_specs=tuple(pl.BlockSpec(s, lambda i, n=len(s): (0,) * n) for s in shapes),
        compiler_params=pltpu.CompilerParams(vmem_limit_bytes=56 * 2**20),
    )(from_up, from_low, *operands)


def ring(value, axis, by):
    n = lax.axis_size(axis)
    return lax.ppermute(value, axis, [(i, (i + by) % n) for i in range(n)])


def swap(value):
    return lax.ppermute(value, "grid", [(0, 1), (1, 0)])


def neighbours(pieces, axis):
    n = lax.axis_size(axis)
    index = lax.axis_index(axis)
    lows = [lax.slice_in_dim(a, a.shape[d] - lo, a.shape[d], axis=d) for a, d, lo, up in pieces]
    ups = [lax.slice_in_dim(a, 0, up, axis=d) for a, d, lo, up in pieces]

    def move(parts, by, keep):
        flat = jnp.concatenate([p.reshape(-1) for p in parts])
        flat = jnp.pad(flat, (0, -flat.size % 1024)).reshape(-1, LANES)
        flat = jnp.where(keep, ring(flat, axis, by), 0.0).reshape(-1)
        out, at = [], 0
        for p in parts:
            out.append(lax.slice_in_dim(flat, at, at + p.size).reshape(p.shape))
            at += p.size
        return out

    return list(zip(move(lows, 1, index > 0), move(ups, -1, index < n - 1)))


def prolong_matrix(m_rows, m_at, x_rows, x_at):
    out = np.zeros((x_rows, m_rows), np.float32)
    where = {m_at(j): j for j in range(m_rows)}
    for i in range(x_rows):
        x = x_at(i)
        m = x // 2
        weights = {m: 1.0} if x % 2 == 0 else {m - 1: -1 / 16, m: 9 / 16, m + 1: 9 / 16, m + 2: -1 / 16}
        for target, weight in weights.items():
            if target in where:
                out[i, where[target]] = weight
    return out


def restrict_matrix(m_rows, m_at, x_rows, x_at):
    out = np.zeros((m_rows, x_rows), np.float32)
    where = {x_at(i): i for i in range(x_rows)}
    for j in range(m_rows):
        m = m_at(j)
        for target, weight in {2 * m - 1: 0.25, 2 * m: 0.5, 2 * m + 1: 0.25}.items():
            if target in where:
                out[j, where[target]] = weight
    return out


def body(
    fine_now, fine_prev, fine_mu, fine_lam, fine_rho, fine_stretch,
    coarse_now, coarse_prev, coarse_mu, coarse_lam, coarse_rho, fine_ghost, coarse_ghost,
):
    g = lax.axis_index("grid")
    upper = g == 0
    wide = lambda a, b: jnp.concatenate([a, b], axis=-1)
    stiff = fine_mu[7] * fine_stretch[7]
    flex = 2.0 / coarse_mu[0]
    low, up = pack(
        (fine_now, fine_mu, fine_lam, fine_rho, fine_stretch, fine_prev, fine_ghost),
        (coarse_now, coarse_mu, coarse_lam, coarse_rho, coarse_prev, coarse_ghost),
    )
    from_up, from_low = ring(low, "gy", -1), ring(up, "gy", 1)
    fine_coef, coarse_coef = coefficients((fine_mu, fine_lam, fine_rho), (coarse_mu, coarse_lam, coarse_rho))
    cut = lambda a, start, size: lax.dynamic_slice_in_dim(a, start, size, axis=1)
    near = near_base(g)
    near_c = 6 * (1 - g)
    fine_z = swap(cut(fine_now, near, 4)), swap(cut(jnp.concatenate([fine_coef, fine_stretch[None]]), near_c, 2))
    coarse_z = swap(cut(coarse_now, near, 4)), swap(cut(coarse_coef, near_c, 2))
    (fine_side, fine_p4, fine_g4, fine_s4, coarse_side, coarse_p4, coarse_g4, coarse_s4, low, up) = unpack(
        from_up, from_low, (fine_now, fine_coef, fine_stretch), (coarse_now, coarse_coef)
    )
    from_up, from_low = ring(low, "gx", -1), ring(up, "gx", 1)
    fine_zside, coarse_zside = swap(cut(fine_side, near, 4)), swap(cut(coarse_side, near, 4))
    z_up, z_low = swap(from_up[:X_NEAR]), swap(from_low[:X_NEAR])
    msgs = (from_low, from_up, z_low, z_up)
    coarse_step, coarse_edge = wave(
        coarse_now, coarse_coef, coarse_coef[0], *coarse_z, coarse_side, coarse_zside, *msgs, coarse_prev, coarse_p4,
        0, X_FINE, X_NEAR,
    )
    fine_step, fine_edge = wave(
        fine_now, fine_coef, fine_stretch, *fine_z, fine_side, fine_zside, *msgs, fine_prev, fine_p4, 6, 0, X_NEAR
    )

    plane_fine = wide(fine_step[:, 7], fine_edge[:, 1])
    above_fine = wide(fine_step[:, 6], fine_edge[:, 0])
    plane_coarse = wide(coarse_step[:, 0], coarse_edge[:, 0])
    below_coarse = wide(coarse_step[:, 1], coarse_edge[:, 1])
    stiff = wide(stiff, fine_s4)
    flex = wide(flex, coarse_s4)
    fine_planes = jnp.concatenate(
        [plane_fine + above_fine, stiff * (wide(fine_ghost, fine_g4) - above_fine), stiff[None]]
    )
    coarse_planes = jnp.concatenate(
        [plane_coarse + below_coarse, plane_coarse + wide(coarse_ghost, coarse_g4), flex[None]]
    )
    (fl, fu), (cl, cu) = neighbours([(fine_planes, 1, 5, 4), (coarse_planes, 1, 3, 4)], "gx")
    pad = lambda a, n, side: jnp.pad(a, ((0, 0), (n, 0) if side else (0, n), (0, 0)))
    fine_planes = jnp.concatenate([pad(fl, 3, 1), fine_planes, pad(fu, 4, 0)], axis=1)
    coarse_planes = jnp.concatenate([pad(cl, 1, 1), coarse_planes, cu], axis=1)
    fine_other, coarse_other = swap(fine_planes), swap(coarse_planes)
    fine_planes = jnp.where(upper, fine_other, fine_planes)
    coarse_planes = jnp.where(upper, coarse_planes, coarse_other)

    fine_rows, fine_cols = fine_planes.shape[1:]
    coarse_rows, coarse_cols = coarse_planes.shape[1:]
    at_rows = (lambda i: i - 4, lambda i: i - 8)
    cyclic = lambda n: lambda i: i if i < n - LANES // 2 else i - n
    at_cols = (cyclic(coarse_cols), cyclic(fine_cols))
    px = prolong_matrix(coarse_rows, at_rows[0], fine_rows, at_rows[1])
    py = prolong_matrix(coarse_cols, at_cols[0], fine_cols, at_cols[1])
    rx = restrict_matrix(coarse_rows, at_rows[0], fine_rows, at_rows[1])
    ry = restrict_matrix(coarse_cols, at_cols[0], fine_cols, at_cols[1])
    both = lambda mx, my, v: jnp.einsum(
        "ax,nxb->nab", mx, jnp.einsum("nxy,by->nxb", v, my, precision=HIGHEST), precision=HIGHEST
    )
    u, w, s = fine_planes[:3], fine_planes[3:6], fine_planes[6]
    p, q, f = coarse_planes[:3], coarse_planes[3:6], coarse_planes[6]
    start = jnp.where(upper, p - both(rx, ry, w) * f, q)
    end = p - both(rx, ry, s * (both(px, py, start) - u)) * f
    fine_plane = both(px, py, end)[:, 8:-8, :512]
    coarse_plane = end[:, 4:-4, :256]
    fine_out = jnp.where(upper, fine_step[:, 7], fine_plane)
    coarse_out = jnp.where(upper, coarse_plane, coarse_step[:, 0])
    fine_next = jnp.concatenate([fine_step[:, :7], fine_out[:, None]], axis=1)
    coarse_next = jnp.concatenate([coarse_out[:, None], coarse_step[:, 1:]], axis=1)
    return fine_next, coarse_next


def solution(mesh):
    block = P(None, "grid", "gx", "gy")
    scalar = P("grid", "gx", "gy")
    plane = P(None, "gx", "gy")
    return jax.shard_map(
        body,
        mesh=mesh,
        in_specs=(block, block, scalar, scalar, scalar, scalar, block, block, scalar, scalar, scalar, plane, plane),
        out_specs=(block, block),
        check_vma=False,
    )
```

```python
import functools

import jax
import jax.numpy as jnp
import numpy as np
from jax import lax
from jax.experimental import pallas as pl
from jax.experimental.pallas import tpu as pltpu
from jax.sharding import PartitionSpec as P

DT2 = 0.09
DT4 = 0.09 * 0.09 / 12.0
LANES = 128
C1, C2 = 4, 5
HIGHEST = lax.Precision.HIGHEST


def derivative_matrix():
    w = np.zeros((256, 256), np.float32)
    first = {-2: 1.0, -1: -8.0, 1: 8.0, 2: -1.0}
    second = {-2: -1.0, -1: 16.0, 0: -30.0, 1: 16.0, 2: -1.0}
    for lane in range(LANES):
        for base, weights in ((0, first), (LANES, second)):
            for offset, weight in weights.items():
                source = lane + offset
                row = source if 0 <= source < LANES else LANES + source % LANES
                w[row, base + lane] += weight
    return w


def diff1(f):
    return 8.0 * (f(1) - f(-1)) - (f(2) - f(-2))


def diff2(f, centre30):
    return 16.0 * (f(1) + f(-1)) - (f(2) + f(-2)) - centre30


def near_base(g):
    return 4 * (1 - g)


def wave_kernel(
    rows, tiles, stretched, edge_k, *refs,
):
    (now_hbm, coef_hbm, stretch_hbm, znow_hbm, zcoef_hbm, side_hbm, zside_hbm,
     low_ref, up_ref, zlow_ref, zup_ref, prev_hbm, prev4_ref, ghost_ref, ghost4_ref, stiff_ref, stiff4_ref, w_ref,
     step_hbm, plane_ref, prev_ref, step_ref, edge_ref, now, acc, coef, dy, dyy, bb, ee, lhs, sem, out_sem) = refs
    g = lax.axis_index("grid")
    gx = lax.axis_index("gx")
    ext = rows + 16
    n_coef = 3 if stretched else 2
    own, own_c = 2 + 4 * g, 4 * g
    zed, zed_c = 10 - 8 * g, 8 - 6 * g
    core = pl.ds(8, rows)

    def fetches(t):
        lanes = pl.ds(t * LANES, LANES) if isinstance(t, int) else pl.ds(pl.multiple_of(t * LANES, LANES), LANES)
        pairs = [
            (now_hbm.at[:, :, :, lanes], now.at[:, pl.ds(own, 8), t, core]),
            (znow_hbm.at[:, :, :, lanes], now.at[:, pl.ds(zed, 4), t, core]),
            (coef_hbm.at[:, :, :, lanes], coef.at[pl.ds(0, 2), pl.ds(own_c, 8), t, core]),
            (zcoef_hbm.at[:, :, :, lanes], coef.at[:, pl.ds(zed_c, 2), t, core]),
        ]
        if stretched:
            pairs.append((stretch_hbm.at[:, :, lanes], coef.at[2, pl.ds(own_c, 8), t, core]))
        return [pltpu.make_async_copy(src, dst, sem.at[t, i]) for i, (src, dst) in enumerate(pairs)]

    def side_fetches():
        pairs = [
            (side_hbm.at[pl.ds(0, 3)], now.at[:, pl.ds(own, 8), tiles, core]),
            (zside_hbm.at[pl.ds(0, 3)], now.at[:, pl.ds(zed, 4), tiles, core]),
            (side_hbm.at[pl.ds(3, n_coef)], coef.at[:, pl.ds(own_c, 8), tiles, core]),
            (zside_hbm.at[pl.ds(3, n_coef)], coef.at[:, pl.ds(8 - 8 * g, 4), tiles, core]),
        ]
        return [pltpu.make_async_copy(src, dst, sem.at[tiles, i]) for i, (src, dst) in enumerate(pairs)]

    prev_copy = pltpu.make_async_copy(prev_hbm, prev_ref, sem.at[tiles, 4])
    for copy in side_fetches() + [copy for t in range(tiles) for copy in fetches(t)] + [prev_copy]:
        copy.start()
    for field in (now, acc):
        for z in (0, 1, 14, 15):
            field[:, z] = jnp.zeros((3, tiles + 1, ext, LANES), jnp.float32)
    for z in (0, 1, 14, 15):
        dy[:, z] = jnp.zeros((3, ext, LANES), jnp.float32)
        ee[z] = jnp.zeros((ext, LANES), jnp.float32)
    near = near_base(g)
    n_now, width = 6 * (tiles + 1), tiles + 1
    n_blocks = n_now + n_coef * width
    last = lax.axis_size("gx") - 1
    for ref, keep, at_now, at_coef in ((low_ref, gx > 0, 4, 6), (up_ref, gx < last, rows + 8, rows + 8)):
        zref = zlow_ref if ref is low_ref else zup_ref
        groups = ((ref, 0, near), (ref, n_blocks, 4 - near), (zref, 0, 8 - 8 * g))
        for source, base, layer in groups:
            first = layer if source is zref else layer + 4 * g
            for t in range(width):
                for c in range(3):
                    for i in range(2):
                        v = jnp.where(keep, source[base + (c * 2 + i) * width + t], 0.0)
                        for h in range(2):
                            now[c, first + 2 + 2 * i + h, t, pl.ds(at_now, 4), :] = v[4 * h : 4 * h + 4]
                for c in range(n_coef):
                    v = jnp.where(keep, source[base + n_now + c * width + t], 0.0)
                    for h in range(4):
                        coef[c, first + h, t, pl.ds(at_coef, 2), :] = v[2 * h : 2 * h + 2]
    for copy in side_fetches() + fetches(0):
        copy.wait()

    low_half = lax.broadcasted_iota(jnp.int32, (ext, LANES), 1) < 64

    def y_stage(src, t, z0, chunk):
        after = jnp.where(t == tiles, 0, t + 1)
        before = jnp.where(t == 0, tiles, t - 1)
        n = chunk * 3 * ext
        for k in range(chunk):
            for c in range(3):
                z = z0 + k
                at = pl.ds((k * 3 + c) * ext, ext)
                at_low = pl.ds(n + (k * 3 + c) * ext, ext)
                side = jnp.where(low_half, src[c, z + 2, after], src[c, z + 2, before])
                for h, v in enumerate((src[c, z + 2, t], side)):
                    high = v.astype(jnp.bfloat16)
                    lanes = pl.ds(h * LANES, LANES)
                    lhs[at, lanes] = high
                    lhs[at_low, lanes] = (v - high.astype(jnp.float32)).astype(jnp.bfloat16)
        out = jnp.dot(lhs[pl.ds(0, 2 * n), :], w_ref[...], preferred_element_type=jnp.float32)
        out = out[:n] + out[n:]
        for k in range(chunk):
            for c in range(3):
                r0 = (k * 3 + c) * ext
                dy[c, z0 + k + 2] = out[r0 : r0 + ext, :LANES]
                dyy[c, z0 + k] = out[r0 : r0 + ext, LANES:]

    def mid_stage(src, t, z):
        for r in range(0, ext, 8):
            at = pl.ds(r, 8)
            bb[z, at, :] = diff1(lambda o: src[2, z + 2 + o, t, at, :])
        for r in range(6, ext - 2, 8):
            along = diff1(lambda o: src[0, z + 2, t, pl.ds(r + o, 8), :])
            ee[z + 2, pl.ds(r, 8), :] = along + dy[1, z + 2, pl.ds(r, 8), :]

    def operator(src, t, z, r):
        at = pl.ds(r, 8)
        c1 = coef[0, z, t, at, :]
        c2 = coef[1, z, t, at, :]
        twelfth = 1.0 / 12.0
        laps, xx, zz = [], [], []
        for c in range(3):
            c30 = 30.0 * src[c, z + 2, t, at, :]
            xx.append(diff2(lambda o: src[c, z + 2, t, pl.ds(r + o, 8), :], c30))
            zz.append(diff2(lambda o: src[c, z + 2 + o, t, at, :], c30))
        yy = [dyy[c, z, at, :] for c in range(3)]
        xy_y = diff1(lambda o: dy[1, z + 2, pl.ds(r + o, 8), :])
        xz_z = diff1(lambda o: bb[z, pl.ds(r + o, 8), :])
        xy_x = diff1(lambda o: dy[0, z + 2, pl.ds(r + o, 8), :])
        yz_z = diff1(lambda o: dy[2, z + 2 + o, at, :])
        z_of = diff1(lambda o: ee[z + 2 + o, at, :])
        if stretched:
            s = coef[2, z, t, at, :]
            s2 = s * s
            zz = [s2 * v for v in zz]
            xz_z, yz_z, z_of = s * xz_z, s * yz_z, s * z_of
        laps = [xx[c] + yy[c] + zz[c] for c in range(3)]
        return (
            c1 * laps[0] + c2 * (xx[0] + twelfth * (xy_y + xz_z)),
            c1 * laps[1] + c2 * (yy[1] + twelfth * (xy_x + yz_z)),
            c1 * laps[2] + c2 * (zz[2] + twelfth * z_of),
        )

    def loop(n, f):
        lax.fori_loop(0, n, lambda i, carry: (f(i), carry)[1], 0)

    def first_pass(t):
        @pl.when(t < tiles - 1)
        def _():
            for copy in fetches(t + 1):
                copy.wait()

        loop(12 // C1, lambda i: y_stage(now, t, C1 * i, C1))
        loop(12, lambda z: mid_stage(now, t, z))

        def layer(i):
            z = i + 2 * g
            for r in range(6, ext - 2, 8):
                for c, value in enumerate(operator(now, t, z, r)):
                    acc[c, z + 2, t, pl.ds(r, 8), :] = value

        loop(10, layer)

    loop(tiles + 1, first_pass)

    def finish(t, z, r, previous, store):
        at = pl.ds(r, 8)
        for c, value in enumerate(operator(acc, t, z, r)):
            total = 2.0 * now[c, z + 2, t, at, :] - previous(c) + DT2 * acc[c, z + 2, t, at, :] + DT4 * value
            store(c, total)

    prev_copy.wait()
    stores = []
    for t in range(tiles + 1):
        if t < tiles:
            loop(10 // C2, lambda i: y_stage(acc, t, C2 * i + 2 * g, C2))
            loop(10, lambda i: mid_stage(acc, t, i + 2 * g))
        else:
            from_k = 4 if edge_k else 0
            y_stage(acc, t, from_k + 4 * g, 4)
            loop(4, lambda i: mid_stage(acc, t, from_k + i + 4 * g))
        if t < tiles:
            lanes = pl.ds(t * LANES, LANES)

            def layer(k):
                z = k + 4 * g
                for r in range(8, rows + 8, 8):
                    at = pl.ds(r - 8, 8)

                    def store(c, value):
                        step_ref[c, k, at, lanes] = value

                    finish(t, z, r, lambda c: prev_ref[c, k, at, lanes], store)

            loop(8, layer)
            stores.append(pltpu.make_async_copy(step_ref.at[:, :, :, lanes], step_hbm.at[:, :, :, lanes], out_sem.at[t]))
            stores[-1].start()
        else:

            def layer(i):
                z = edge_k + i + 4 * g
                for r in range(8, rows + 8, 8):
                    at = pl.ds(r - 8, 8)

                    def store(c, value):
                        edge_ref[c, i, at, :] = value

                    finish(t, z, r, lambda c: prev4_ref[c, i, at, :], store)

            loop(2, layer)


    for t in range(tiles + 1):
        lanes = pl.ds(t * LANES, LANES)
        side = t == tiles
        stiff = stiff4_ref[...] if side else stiff_ref[:, lanes]
        for c in range(3):
            ghost = ghost4_ref[c] if side else ghost_ref[c, :, lanes]
            first, second = [edge_ref[c, i] if side else step_ref[c, edge_k + i, :, lanes] for i in range(2)]
            plane_ref[c, :, lanes] = first + second
            plane_ref[3 + c, :, lanes] = stiff * (ghost - first) if stretched else first + ghost
        plane_ref[6, :, lanes] = stiff
    for copy in stores:
        copy.wait()


def wave(
    now, coef, stretch, znow, zcoef, side, zside, low, up, zlow, zup, prev, prev4, ghost, ghost4, stiff, stiff4, edge_k
):
    rows, cols = prev.shape[2:]
    tiles = cols // LANES
    ext = rows + 16
    stretched = zcoef.shape[0] == 3
    vmem = pl.BlockSpec(memory_space=pltpu.VMEM)
    hbm = pl.BlockSpec(memory_space=pl.ANY)
    f32 = jnp.float32
    units = 3 * (10 * (ext - 8) // 8 * (tiles + 1) + rows * tiles)
    return pl.pallas_call(
        functools.partial(wave_kernel, rows, tiles, stretched, edge_k),
        out_shape=(
            jax.ShapeDtypeStruct((3, 8, rows, cols), f32),
            jax.ShapeDtypeStruct((7, rows, cols + LANES), f32),
        ),
        in_specs=[hbm] * 7 + [vmem] * 4 + [hbm] + [vmem] * 6,
        out_specs=(hbm, vmem),
        scratch_shapes=[
            pltpu.VMEM((3, 8, rows, cols), f32),
            pltpu.VMEM((3, 8, rows, cols), f32),
            pltpu.VMEM((3, 2, rows, LANES), f32),
            pltpu.VMEM((3, 16, tiles + 1, ext, LANES), f32),
            pltpu.VMEM((3, 16, tiles + 1, ext, LANES), f32),
            pltpu.VMEM((zcoef.shape[0], 12, tiles + 1, ext, LANES), f32),
            pltpu.VMEM((3, 16, ext, LANES), f32),
            pltpu.VMEM((3, 12, ext, LANES), f32),
            pltpu.VMEM((12, ext, LANES), f32),
            pltpu.VMEM((16, ext, LANES), f32),
            pltpu.VMEM((max(C1, C2) * 6 * ext, 256), jnp.bfloat16),
            pltpu.SemaphoreType.DMA((tiles + 1, 5)),
            pltpu.SemaphoreType.DMA((tiles,)),
        ],
        compiler_params=pltpu.CompilerParams(vmem_limit_bytes=58 * 2**20),
        cost_estimate=pl.CostEstimate(flops=units * 100000, bytes_accessed=10 * 2**20, transcendentals=0),
    )(
        now, coef, stretch, znow, zcoef, side, zside, low, up, zlow, zup, prev, prev4, ghost, ghost4, stiff, stiff4,
        jnp.asarray(derivative_matrix(), jnp.bfloat16),
    )


def slots(widths):
    out, tile, lane = [], 0, 0
    for width in widths:
        if lane + width > LANES:
            tile, lane = tile + 1, 0
        out.append((tile, lane))
        lane += width
    return out, tile + 1


FINE_HALO = ((9, 8), (7, 6), (5, 4), (5, 4), (5, 4))
COARSE_HALO = ((7, 8), (5, 6), (3, 4), (3, 4), (3, 4))


def items_of(halo, n_coef):
    kinds = [0] * 24 + [1] * (8 * n_coef) + [2] * 6 + [3] * 3 + [4]
    halos = [halo[k] for k in kinds]
    places, n_tiles = slots([max(h) for h in halos])
    return halos, places, n_tiles


def lane_between(lane, first, width):
    first = first % LANES
    if first + width <= LANES:
        return (lane >= first) & (lane < first + width)
    return (lane >= first) | (lane < first + width - LANES)


def pack_kernel(*refs):
    fine_in, coarse_in, (low_ref, up_ref) = refs[:14], refs[14:26], refs[26:]
    block = 0
    for rows, ins, halo, n_coef in ((64, fine_in, FINE_HALO, 3), (32, coarse_in, COARSE_HALO, 2)):
        halos, places, n_tiles = items_of(halo, n_coef)
        lane = lax.broadcasted_iota(jnp.int32, (rows, LANES), 1)
        half = lane < 64
        pick = lambda i, *at: jnp.where(half, ins[2 * i][at], ins[2 * i + 1][at])
        scale = 12.0 if n_coef == 3 else 48.0

        def coefficients(z):
            mu, lam = pick(1, z), pick(2, z)
            inverse = 1.0 / (scale * pick(3, z))
            out = [mu * inverse, (mu + lam) * inverse]
            return out + [pick(4, z)] if n_coef == 3 else out

        values = [lambda c=c, z=z: pick(0, c, z) for c in range(3) for z in range(8)]
        held = {}

        def coefficient(c, z):
            if z not in held:
                held[z] = coefficients(z)
            return held[z][c]

        values += [lambda c=c, z=z: coefficient(c, z) for z in range(8) for c in range(n_coef)]
        at = 5 if n_coef == 3 else 4
        values += [lambda c=c, z=z: pick(at, c, z) for c in range(3) for z in range(2)]
        values += [lambda c=c: pick(at + 1, c) for c in range(3)]
        if n_coef == 3:
            values.append(lambda: pick(1, 7) * pick(4, 7))
        else:
            values.append(lambda: 2.0 / pick(1, 0))
        for tile in range(n_tiles):
            low = jnp.zeros((rows, LANES), jnp.float32)
            up = jnp.zeros((rows, LANES), jnp.float32)
            for value, (lo, hi), (home, first) in zip(values, halos, places):
                if home == tile:
                    turned = value()
                    turned = pltpu.roll(turned, first, 1) if first else turned
                    low = jnp.where(lane_between(lane, first, hi), turned, low)
                    up = jnp.where(lane_between(lane, first - lo, lo), turned, up)
            for r in range(rows // 8):
                low_ref[block] = low[8 * r : 8 * r + 8]
                up_ref[block] = up[8 * r : 8 * r + 8]
                block += 1


Y_BLOCKS = 8 * items_of(FINE_HALO, 3)[2] + 4 * items_of(COARSE_HALO, 2)[2]


def pack(fine, coarse):
    specs, operands = [], []
    for arrays, layer_of_prev, tiles in ((fine, 3, 4), (coarse, 0, 2)):
        for i, a in enumerate(arrays):
            block = list(a.shape[:-1]) + [LANES]
            at = [0] * a.ndim
            if i == len(arrays) - 2:
                block[1], at[1] = 2, layer_of_prev
            for tile in (0, tiles - 1):
                where = tuple(at[:-1] + [tile])
                specs.append(pl.BlockSpec(tuple(block), lambda i, where=where: where))
                operands.append(a)
    out = jax.ShapeDtypeStruct((Y_BLOCKS, 8, LANES), jnp.float32)
    whole = pl.BlockSpec((Y_BLOCKS, 8, LANES), lambda i: (0, 0, 0))
    return pl.pallas_call(
        pack_kernel, grid=(1,), out_shape=(out, out), in_specs=specs, out_specs=(whole, whole),
        compiler_params=pltpu.CompilerParams(vmem_limit_bytes=56 * 2**20),
    )(*operands)


def coefficient_kernel(scales, *refs):
    n = len(scales)
    for i, scale in enumerate(scales):
        mu, lam, rho = refs[3 * i : 3 * i + 3]
        out = refs[3 * n + 1 + i]

        def layer(z, carry, mu=mu, lam=lam, rho=rho, out=out, scale=scale):
            inverse = 1.0 / (scale * rho[z])
            out[0, z] = mu[z] * inverse
            out[1, z] = (mu[z] + lam[z]) * inverse
            return carry

        lax.fori_loop(0, 8, layer, 0)
    stretch, stiff, flex = refs[3 * n], refs[-2], refs[-1]
    stiff[...] = refs[0][7] * stretch[0]
    flex[...] = 2.0 / refs[3][0]


def coefficients(fine, coarse, stretch):
    vmem = pl.BlockSpec(memory_space=pltpu.VMEM)
    shapes = [(2,) + a[0].shape for a in (fine, coarse)] + [a[0].shape[1:] for a in (fine, coarse)]
    return pl.pallas_call(
        functools.partial(coefficient_kernel, (12.0, 48.0)),
        out_shape=tuple(jax.ShapeDtypeStruct(a, jnp.float32) for a in shapes),
        in_specs=[vmem] * 7, out_specs=(vmem,) * 4,
        compiler_params=pltpu.CompilerParams(vmem_limit_bytes=56 * 2**20),
        cost_estimate=pl.CostEstimate(flops=10**7, bytes_accessed=7 * 2**20, transcendentals=0),
    )(*fine, *coarse, stretch)


def unpack_kernel(*refs):
    from_up, from_low = refs[:2]
    fine_edges, coarse_edges = refs[2:8], refs[8:12]
    fine_out, coarse_out, fine_msgs, coarse_msgs = refs[12:16], refs[16:20], refs[20:22], refs[22:]
    g = lax.axis_index("grid")
    gy = lax.axis_index("gy")
    keep_low, keep_up = gy > 0, gy < lax.axis_size("gy") - 1
    near = near_base(g)
    block0 = 0
    for rows, halo, n_coef, outs in ((64, FINE_HALO, 3, fine_out), (32, COARSE_HALO, 2, coarse_out)):
        halos, places, n_tiles = items_of(halo, n_coef)
        lane = lax.broadcasted_iota(jnp.int32, (rows, LANES), 1)
        side_ref, prev_ref, ghost_ref, stiff_ref = outs
        stores = [lambda v, c=c, z=z: side_ref.__setitem__((c, z), v) for c in range(3) for z in range(8)]
        stores += [lambda v, c=c, z=z: side_ref.__setitem__((3 + c, z), v) for z in range(8) for c in range(n_coef)]
        stores += [lambda v, c=c, z=z: prev_ref.__setitem__((c, z), v) for c in range(3) for z in range(2)]
        stores += [lambda v, c=c: ghost_ref.__setitem__((c,), v) for c in range(3)]
        stores += [lambda v: stiff_ref.__setitem__((Ellipsis,), v)]
        tiles = []
        for tile in range(n_tiles):
            at = pl.ds(block0 + tile * rows // 8, rows // 8)
            tiles.append((from_up[at].reshape(rows, LANES), from_low[at].reshape(rows, LANES)))
        block0 += n_tiles * rows // 8
        for store, (lo, hi), (home, first) in zip(stores, halos, places):
            up, low = tiles[home]
            both = jnp.where(lane_between(lane, first, hi), up, low)
            both = pltpu.roll(both, LANES - first, 1) if first else both
            valid = ((lane < hi) & keep_up) | ((lane >= LANES - lo) & keep_low)
            store(jnp.where(valid, both, 0.0))
    for rows, width, n_coef, outs, edges, msgs in (
        (64, 5, 3, fine_out, fine_edges, fine_msgs), (32, 3, 2, coarse_out, coarse_edges, coarse_msgs)
    ):
        side_ref = outs[0]
        half_blocks = (6 + n_coef) * width
        first_rows, last_rows = edges[0::2], edges[1::2]
        for msg, edge, is_last in ((msgs[0], first_rows, False), (msgs[1], last_rows, True)):
            for start, layer0 in ((0, near), (half_blocks, 4 - near)):
                for t in range(width):
                    lanes = pl.ds(t * LANES, LANES)

                    def rows_of(kind, c, z, count):
                        if t == width - 1:
                            tile = pl.ds(rows - 8, 8) if is_last else pl.ds(0, 8)
                            v = side_ref[3 * kind + c, z, tile, :]
                        elif kind == 0:
                            v = edge[0][c, z, :, lanes]
                        elif c < 2:
                            v = edge[1][c, z, :, lanes]
                        else:
                            v = edge[2][z, :, lanes]
                        return v[8 - count :] if is_last else v[:count]

                    for c in range(3):
                        for i in range(2):
                            parts = [rows_of(0, c, layer0 + 2 * i + h, 4) for h in range(2)]
                            msg[start + (c * 2 + i) * width + t] = jnp.concatenate(parts, axis=0)
                    for c in range(n_coef):
                        parts = [rows_of(1, c, layer0 + h, 2) for h in range(4)]
                        msg[start + (6 + c) * width + t] = jnp.concatenate(parts, axis=0)


X_FINE = 9 * 5
X_COARSE = 8 * 3


def unpack(from_up, from_low, fine, coarse):
    vmem = pl.BlockSpec(memory_space=pltpu.VMEM)
    specs, operands = [], []
    whole = pl.BlockSpec((Y_BLOCKS, 8, LANES), lambda i: (0, 0, 0))
    for arrays in (fine, coarse):
        for a in arrays:
            block = list(a.shape)
            block[-2] = 8
            for tile in (0, a.shape[-2] // 8 - 1):
                where = tuple([0] * (a.ndim - 2) + [tile, 0])
                specs.append(pl.BlockSpec(tuple(block), lambda i, where=where: where))
                operands.append(a)
    shapes = []
    for rows, n_coef in ((64, 3), (32, 2)):
        shapes += [(3 + n_coef, 8, rows, LANES), (3, 2, rows, LANES), (3, rows, LANES), (rows, LANES)]
    shapes += [(2 * X_FINE, 8, LANES)] * 2 + [(2 * X_COARSE, 8, LANES)] * 2
    return pl.pallas_call(
        unpack_kernel, grid=(1,),
        out_shape=tuple(jax.ShapeDtypeStruct(s, jnp.float32) for s in shapes),
        in_specs=[whole, whole] + specs,
        out_specs=tuple(pl.BlockSpec(s, lambda i, n=len(s): (0,) * n) for s in shapes),
        compiler_params=pltpu.CompilerParams(vmem_limit_bytes=56 * 2**20),
    )(from_up, from_low, *operands)


def ring(value, axis, by):
    n = lax.axis_size(axis)
    return lax.ppermute(value, axis, [(i, (i + by) % n) for i in range(n)])


def swap(value):
    return lax.ppermute(value, "grid", [(0, 1), (1, 0)])


def neighbours(pieces, axis):
    n = lax.axis_size(axis)
    index = lax.axis_index(axis)
    lows = [lax.slice_in_dim(a, a.shape[d] - lo, a.shape[d], axis=d) for a, d, lo, up in pieces]
    ups = [lax.slice_in_dim(a, 0, up, axis=d) for a, d, lo, up in pieces]

    def move(parts, by, keep):
        flat = jnp.concatenate([p.reshape(-1) for p in parts])
        flat = jnp.pad(flat, (0, -flat.size % 1024)).reshape(-1, LANES)
        flat = jnp.where(keep, ring(flat, axis, by), 0.0).reshape(-1)
        out, at = [], 0
        for p in parts:
            out.append(lax.slice_in_dim(flat, at, at + p.size).reshape(p.shape))
            at += p.size
        return out

    return list(zip(move(lows, 1, index > 0), move(ups, -1, index < n - 1)))


def prolong_matrix(m_rows, m_at, x_rows, x_at):
    out = np.zeros((x_rows, m_rows), np.float32)
    where = {m_at(j): j for j in range(m_rows)}
    for i in range(x_rows):
        x = x_at(i)
        m = x // 2
        weights = {m: 1.0} if x % 2 == 0 else {m - 1: -1 / 16, m: 9 / 16, m + 1: 9 / 16, m + 2: -1 / 16}
        for target, weight in weights.items():
            if target in where:
                out[i, where[target]] = weight
    return out


def restrict_matrix(m_rows, m_at, x_rows, x_at):
    out = np.zeros((m_rows, x_rows), np.float32)
    where = {x_at(i): i for i in range(x_rows)}
    for j in range(m_rows):
        m = m_at(j)
        for target, weight in {2 * m - 1: 0.25, 2 * m: 0.5, 2 * m + 1: 0.25}.items():
            if target in where:
                out[j, where[target]] = weight
    return out


def times(rows, w_ref):
    n = rows.shape[0]
    high = rows.astype(jnp.bfloat16)
    low = (rows - high.astype(jnp.float32)).astype(jnp.bfloat16)
    out = jnp.dot(jnp.concatenate([high, low], axis=0), w_ref[...], preferred_element_type=jnp.float32)
    return out[:n] + out[n:]


def interface_kernel(*refs):
    fine, coarse, (py_ref, ry_ref) = refs[0:6], refs[6:12], refs[12:14]
    (out_fine, out_coarse, fine_plane, coarse_plane, tall, short, sem) = refs[16:]
    g = lax.axis_index("grid")
    gx = lax.axis_index("gx")
    lower = g == 1
    keep_low, keep_up = gx > 0, gx < lax.axis_size("gx") - 1
    fine_rows, coarse_rows = tall.shape[1] - 16, short.shape[1]
    half = fine_rows // 2

    def grown(parts, i, own):
        core, low, up = [jnp.where(own, parts[k][i], parts[3 + k][i]) for k in range(3)]
        return jnp.concatenate([jnp.where(keep_low, low, 0.0), core, jnp.where(keep_up, up, 0.0)], axis=0)

    def prolong(planes):
        whole = []
        for plane in planes:
            parts = []
            for t in range(plane.shape[1] // LANES):
                short[t] = plane[:, t * LANES : (t + 1) * LANES]
                at = lambda i: short[t, pl.ds(i, half), :]
                tall[t, pl.ds(0, half, stride=2), :] = at(4)
                tall[t, pl.ds(1, half, stride=2), :] = (9.0 * (at(4) + at(5)) - (at(3) + at(6))) * 0.0625
                parts.append(tall[t, pl.ds(0, fine_rows), :])
            whole.append(jnp.concatenate(parts, axis=1))
        out = times(jnp.concatenate(whole, axis=0), py_ref)
        return [out[c * fine_rows : (c + 1) * fine_rows] for c in range(3)]

    def restrict(planes):
        whole = []
        for plane in planes:
            parts = []
            for t in range(plane.shape[1] // LANES):
                tall[t, pl.ds(8, fine_rows), :] = plane[:, t * LANES : (t + 1) * LANES]
                at = lambda i: tall[t, pl.ds(i, half, stride=2), :]
                parts.append(0.25 * (at(7) + at(9)) + 0.5 * at(8))
            whole.append(jnp.concatenate(parts, axis=1))
        out = times(jnp.concatenate(whole, axis=0), ry_ref)
        gap = jnp.zeros((4, out.shape[1]), jnp.float32)
        return [jnp.concatenate([gap, out[c * half : (c + 1) * half], gap], axis=0) for c in range(3)]

    tall[...] = jnp.zeros(tall.shape, jnp.float32)
    own_coarse = jnp.logical_not(lower)
    s, f = grown(fine, 6, lower), grown(coarse, 6, own_coarse)
    u, w = [[grown(fine, 3 * k + c, lower) for c in range(3)] for k in range(2)]
    p, q = [[grown(coarse, 3 * k + c, own_coarse) for c in range(3)] for k in range(2)]
    r = restrict(w)
    start = [jnp.where(lower, q[c], p[c] - r[c] * f) for c in range(3)]
    v = prolong(start)
    r = restrict([s * (v[c] - u[c]) for c in range(3)])
    end = [p[c] - r[c] * f for c in range(3)]
    v = prolong(end)
    for c in range(3):
        coarse_plane[c] = end[c][8:-8, : coarse_plane.shape[2]]
        fine_plane[c] = v[c][8:-8, : fine_plane.shape[2]]

    @pl.when(lower)
    def _():
        copy = pltpu.make_async_copy(fine_plane, out_fine.at[:, 7], sem)
        copy.start()
        copy.wait()

    @pl.when(g == 0)
    def _():
        copy = pltpu.make_async_copy(coarse_plane, out_coarse.at[:, 0], sem)
        copy.start()
        copy.wait()


def interface(fine, coarse, fine_step, coarse_step):
    fine_rows, fine_cols = fine[0].shape[1] + 16, fine[0].shape[2]
    coarse_rows, coarse_cols = coarse[0].shape[1] + 16, coarse[0].shape[2]
    cyclic = lambda n: lambda i: i if i < n - LANES // 2 else i - n
    cols = (coarse_cols, cyclic(coarse_cols), fine_cols, cyclic(fine_cols))
    maps = (prolong_matrix(*cols).T, restrict_matrix(*cols).T)
    vmem = pl.BlockSpec(memory_space=pltpu.VMEM)
    hbm = pl.BlockSpec(memory_space=pl.ANY)
    f32 = jnp.float32
    return pl.pallas_call(
        interface_kernel,
        out_shape=tuple(jax.ShapeDtypeStruct(a.shape, f32) for a in (fine_step, coarse_step)),
        in_specs=[vmem] * 14 + [hbm] * 2,
        out_specs=(hbm, hbm),
        input_output_aliases={14: 0, 15: 1},
        scratch_shapes=[
            pltpu.VMEM((3, fine_rows - 16, fine_cols - LANES), f32),
            pltpu.VMEM((3, coarse_rows - 16, coarse_cols - LANES), f32),
            pltpu.VMEM((fine_cols // LANES, fine_rows + 16, LANES), f32),
            pltpu.VMEM((coarse_cols // LANES, coarse_rows, LANES), f32),
            pltpu.SemaphoreType.DMA,
        ],
        compiler_params=pltpu.CompilerParams(vmem_limit_bytes=56 * 2**20),
    )(*fine, *coarse, *[jnp.asarray(m, jnp.bfloat16) for m in maps], fine_step, coarse_step)


def body(
    fine_now, fine_prev, fine_mu, fine_lam, fine_rho, fine_stretch,
    coarse_now, coarse_prev, coarse_mu, coarse_lam, coarse_rho, fine_ghost, coarse_ghost,
):
    g = lax.axis_index("grid")
    low, up = pack(
        (fine_now, fine_mu, fine_lam, fine_rho, fine_stretch, fine_prev, fine_ghost),
        (coarse_now, coarse_mu, coarse_lam, coarse_rho, coarse_prev, coarse_ghost),
    )
    fine_now_z, coarse_now_z, low, up = lax.optimization_barrier((fine_now, coarse_now, low, up))
    from_up, from_low = ring(low, "gy", -1), ring(up, "gy", 1)
    fine_coef, coarse_coef, stiff, flex = coefficients(
        (fine_mu, fine_lam, fine_rho), (coarse_mu, coarse_lam, coarse_rho), fine_stretch[7:]
    )
    cut = lambda a, start, size: lax.dynamic_slice_in_dim(a, start, size, axis=1)
    near = near_base(g)
    near_c = 6 * (1 - g)
    fine_z = swap(cut(fine_now_z, near, 4)), swap(cut(jnp.concatenate([fine_coef, fine_stretch[None]]), near_c, 2))
    coarse_z = swap(cut(coarse_now_z, near, 4)), swap(cut(coarse_coef, near_c, 2))
    (fine_side, fine_p4, fine_g4, fine_s4, coarse_side, coarse_p4, coarse_g4, coarse_s4,
     fine_low, fine_up, coarse_low, coarse_up) = unpack(
        from_up, from_low, (fine_now, fine_coef, fine_stretch), (coarse_now, coarse_coef)
    )

    def x_rings(low, up):
        return ring(up, "gx", 1), ring(low, "gx", -1)

    def x_halos(from_low, from_up):
        n = from_low.shape[0] // 2
        return from_low, from_up, swap(from_low[:n]), swap(from_up[:n])

    def plane_halos(planes):
        from_low, from_up = ring(planes[:, -8:], "gx", 1), ring(planes[:, :8], "gx", -1)
        return planes, from_low, from_up, swap(planes), swap(from_low), swap(from_up)

    coarse_x, fine_x = x_rings(coarse_low, coarse_up), x_rings(fine_low, fine_up)
    coarse_zside, fine_zside = swap(cut(coarse_side, near, 4)), swap(cut(fine_side, near, 4))
    coarse_step, coarse_planes = wave(
        coarse_now, coarse_coef, coarse_coef[0], *coarse_z, coarse_side, coarse_zside, *x_halos(*coarse_x),
        coarse_prev, coarse_p4, coarse_ghost, coarse_g4, flex, coarse_s4, 0,
    )
    coarse_step, coarse_planes, *fine_x = lax.optimization_barrier((coarse_step, coarse_planes, *fine_x))
    coarse_planes = plane_halos(coarse_planes)
    fine_step, fine_planes = wave(
        fine_now, fine_coef, fine_stretch, *fine_z, fine_side, fine_zside, *x_halos(*fine_x),
        fine_prev, fine_p4, fine_ghost, fine_g4, stiff, fine_s4, 6,
    )
    return interface(plane_halos(fine_planes), coarse_planes, fine_step, coarse_step)


def solution(mesh):
    block = P(None, "grid", "gx", "gy")
    scalar = P("grid", "gx", "gy")
    plane = P(None, "gx", "gy")
    return jax.shard_map(
        body,
        mesh=mesh,
        in_specs=(block, block, scalar, scalar, scalar, scalar, block, block, scalar, scalar, scalar, plane, plane),
        out_specs=(block, block),
        check_vma=False,
    )
```

```python
import functools

import jax
import jax.numpy as jnp
import numpy as np
from jax import lax
from jax.experimental import pallas as pl
from jax.experimental.pallas import tpu as pltpu
from jax.sharding import PartitionSpec as P

DT2 = 0.09
DT4 = 0.09 * 0.09 / 12.0
LANES = 128
C1, C2 = 4, 5
HIGHEST = lax.Precision.HIGHEST


def derivative_matrix():
    w = np.zeros((256, 256), np.float32)
    first = {-2: 1.0, -1: -8.0, 1: 8.0, 2: -1.0}
    second = {-2: -1.0, -1: 16.0, 0: -30.0, 1: 16.0, 2: -1.0}
    for lane in range(LANES):
        for base, weights in ((0, first), (LANES, second)):
            for offset, weight in weights.items():
                source = lane + offset
                row = source if 0 <= source < LANES else LANES + source % LANES
                w[row, base + lane] += weight
    return w


def diff1(f):
    return 8.0 * (f(1) - f(-1)) - (f(2) - f(-2))


def diff2(f, centre30):
    return 16.0 * (f(1) + f(-1)) - (f(2) + f(-2)) - centre30


def near_base(g):
    return 4 * (1 - g)


def wave_kernel(
    rows, tiles, stretched, edge_k, *refs,
):
    (now_hbm, coef_hbm, stretch_hbm, znow_hbm, zcoef_hbm, side_hbm, zside_hbm,
     low_ref, up_ref, zlow_ref, zup_ref, prev_hbm, prev4_ref, ghost_ref, ghost4_ref, stiff_ref, stiff4_ref, w_ref,
     step_hbm, plane_ref, prev_ref, step_ref, edge_ref, now, acc, coef, dy, dyy, bb, ee, lhs, sem, out_sem) = refs
    g = lax.axis_index("grid")
    gx = lax.axis_index("gx")
    ext = rows + 16
    n_coef = 3 if stretched else 2
    own, own_c = 2 + 4 * g, 4 * g
    zed, zed_c = 10 - 8 * g, 8 - 6 * g
    core = pl.ds(8, rows)

    def fetches(t):
        lanes = pl.ds(t * LANES, LANES) if isinstance(t, int) else pl.ds(pl.multiple_of(t * LANES, LANES), LANES)
        pairs = [
            (now_hbm.at[:, :, :, lanes], now.at[:, pl.ds(own, 8), t, core]),
            (znow_hbm.at[:, :, :, lanes], now.at[:, pl.ds(zed, 4), t, core]),
            (coef_hbm.at[:, :, :, lanes], coef.at[pl.ds(0, 2), pl.ds(own_c, 8), t, core]),
            (zcoef_hbm.at[:, :, :, lanes], coef.at[:, pl.ds(zed_c, 2), t, core]),
        ]
        if stretched:
            pairs.append((stretch_hbm.at[:, :, lanes], coef.at[2, pl.ds(own_c, 8), t, core]))
        return [pltpu.make_async_copy(src, dst, sem.at[t, i]) for i, (src, dst) in enumerate(pairs)]

    def side_fetches():
        pairs = [
            (side_hbm.at[pl.ds(0, 3)], now.at[:, pl.ds(own, 8), tiles, core]),
            (zside_hbm.at[pl.ds(0, 3)], now.at[:, pl.ds(zed, 4), tiles, core]),
            (side_hbm.at[pl.ds(3, n_coef)], coef.at[:, pl.ds(own_c, 8), tiles, core]),
            (zside_hbm.at[pl.ds(3, n_coef)], coef.at[:, pl.ds(8 - 8 * g, 4), tiles, core]),
        ]
        return [pltpu.make_async_copy(src, dst, sem.at[tiles, i]) for i, (src, dst) in enumerate(pairs)]

    prev_copy = pltpu.make_async_copy(prev_hbm, prev_ref, sem.at[tiles, 4])
    for copy in side_fetches() + [copy for t in range(tiles) for copy in fetches(t)] + [prev_copy]:
        copy.start()
    for field in (now, acc):
        for z in (0, 1, 14, 15):
            field[:, z] = jnp.zeros((3, tiles + 1, ext, LANES), jnp.float32)
    for z in (0, 1, 14, 15):
        dy[:, z] = jnp.zeros((3, ext, LANES), jnp.float32)
        ee[z] = jnp.zeros((ext, LANES), jnp.float32)
    near = near_base(g)
    n_now, width = 6 * (tiles + 1), tiles + 1
    n_blocks = n_now + n_coef * width
    last = lax.axis_size("gx") - 1
    for ref, keep, at_now, at_coef in ((low_ref, gx > 0, 4, 6), (up_ref, gx < last, rows + 8, rows + 8)):
        zref = zlow_ref if ref is low_ref else zup_ref
        groups = ((ref, 0, near), (ref, n_blocks, 4 - near), (zref, 0, 8 - 8 * g))
        for source, base, layer in groups:
            first = layer if source is zref else layer + 4 * g
            for t in range(width):
                for c in range(3):
                    for i in range(2):
                        v = jnp.where(keep, source[base + (c * 2 + i) * width + t], 0.0)
                        for h in range(2):
                            now[c, first + 2 + 2 * i + h, t, pl.ds(at_now, 4), :] = v[4 * h : 4 * h + 4]
                for c in range(n_coef):
                    v = jnp.where(keep, source[base + n_now + c * width + t], 0.0)
                    for h in range(4):
                        coef[c, first + h, t, pl.ds(at_coef, 2), :] = v[2 * h : 2 * h + 2]
    for copy in side_fetches() + fetches(0):
        copy.wait()

    low_half = lax.broadcasted_iota(jnp.int32, (ext, LANES), 1) < 64

    def y_stage(src, t, z0, chunk):
        after = jnp.where(t == tiles, 0, t + 1)
        before = jnp.where(t == 0, tiles, t - 1)
        n = chunk * 3 * ext
        for k in range(chunk):
            for c in range(3):
                z = z0 + k
                at = pl.ds((k * 3 + c) * ext, ext)
                at_low = pl.ds(n + (k * 3 + c) * ext, ext)
                side = jnp.where(low_half, src[c, z + 2, after], src[c, z + 2, before])
                for h, v in enumerate((src[c, z + 2, t], side)):
                    high = v.astype(jnp.bfloat16)
                    lanes = pl.ds(h * LANES, LANES)
                    lhs[at, lanes] = high
                    lhs[at_low, lanes] = (v - high.astype(jnp.float32)).astype(jnp.bfloat16)
        out = jnp.dot(lhs[pl.ds(0, 2 * n), :], w_ref[...], preferred_element_type=jnp.float32)
        out = out[:n] + out[n:]
        for k in range(chunk):
            for c in range(3):
                r0 = (k * 3 + c) * ext
                dy[c, z0 + k + 2] = out[r0 : r0 + ext, :LANES]
                dyy[c, z0 + k] = out[r0 : r0 + ext, LANES:]

    def mid_stage(src, t, z):
        for r in range(0, ext, 8):
            at = pl.ds(r, 8)
            bb[z, at, :] = diff1(lambda o: src[2, z + 2 + o, t, at, :])
        for r in range(6, ext - 2, 8):
            along = diff1(lambda o: src[0, z + 2, t, pl.ds(r + o, 8), :])
            ee[z + 2, pl.ds(r, 8), :] = along + dy[1, z + 2, pl.ds(r, 8), :]

    def operator(src, t, z, r):
        at = pl.ds(r, 8)
        c1 = coef[0, z, t, at, :]
        c2 = coef[1, z, t, at, :]
        twelfth = 1.0 / 12.0
        laps, xx, zz = [], [], []
        for c in range(3):
            c30 = 30.0 * src[c, z + 2, t, at, :]
            xx.append(diff2(lambda o: src[c, z + 2, t, pl.ds(r + o, 8), :], c30))
            zz.append(diff2(lambda o: src[c, z + 2 + o, t, at, :], c30))
        yy = [dyy[c, z, at, :] for c in range(3)]
        xy_y = diff1(lambda o: dy[1, z + 2, pl.ds(r + o, 8), :])
        xz_z = diff1(lambda o: bb[z, pl.ds(r + o, 8), :])
        xy_x = diff1(lambda o: dy[0, z + 2, pl.ds(r + o, 8), :])
        yz_z = diff1(lambda o: dy[2, z + 2 + o, at, :])
        z_of = diff1(lambda o: ee[z + 2 + o, at, :])
        if stretched:
            s = coef[2, z, t, at, :]
            s2 = s * s
            zz = [s2 * v for v in zz]
            xz_z, yz_z, z_of = s * xz_z, s * yz_z, s * z_of
        laps = [xx[c] + yy[c] + zz[c] for c in range(3)]
        return (
            c1 * laps[0] + c2 * (xx[0] + twelfth * (xy_y + xz_z)),
            c1 * laps[1] + c2 * (yy[1] + twelfth * (xy_x + yz_z)),
            c1 * laps[2] + c2 * (zz[2] + twelfth * z_of),
        )

    def loop(n, f):
        lax.fori_loop(0, n, lambda i, carry: (f(i), carry)[1], 0)

    def first_pass(t):
        @pl.when(t < tiles - 1)
        def _():
            for copy in fetches(t + 1):
                copy.wait()

        loop(12 // C1, lambda i: y_stage(now, t, C1 * i, C1))
        loop(12, lambda z: mid_stage(now, t, z))

        def layer(i):
            z = i + 2 * g
            for r in range(6, ext - 2, 8):
                for c, value in enumerate(operator(now, t, z, r)):
                    acc[c, z + 2, t, pl.ds(r, 8), :] = value

        loop(10, layer)

    loop(tiles + 1, first_pass)

    def finish(t, z, r, previous, store):
        at = pl.ds(r, 8)
        for c, value in enumerate(operator(acc, t, z, r)):
            total = 2.0 * now[c, z + 2, t, at, :] - previous(c) + DT2 * acc[c, z + 2, t, at, :] + DT4 * value
            store(c, total)

    prev_copy.wait()
    stores = []
    for t in range(tiles + 1):
        if t < tiles:
            loop(10 // C2, lambda i: y_stage(acc, t, C2 * i + 2 * g, C2))
            loop(10, lambda i: mid_stage(acc, t, i + 2 * g))
        else:
            from_k = 4 if edge_k else 0
            y_stage(acc, t, from_k + 4 * g, 4)
            loop(4, lambda i: mid_stage(acc, t, from_k + i + 4 * g))
        if t < tiles:
            lanes = pl.ds(t * LANES, LANES)

            def layer(k):
                z = k + 4 * g
                for r in range(8, rows + 8, 8):
                    at = pl.ds(r - 8, 8)

                    def store(c, value):
                        step_ref[c, k, at, lanes] = value

                    finish(t, z, r, lambda c: prev_ref[c, k, at, lanes], store)

            loop(8, layer)
            stores.append(pltpu.make_async_copy(step_ref.at[:, :, :, lanes], step_hbm.at[:, :, :, lanes], out_sem.at[t]))
            stores[-1].start()
        else:

            def layer(i):
                z = edge_k + i + 4 * g
                for r in range(8, rows + 8, 8):
                    at = pl.ds(r - 8, 8)

                    def store(c, value):
                        edge_ref[c, i, at, :] = value

                    finish(t, z, r, lambda c: prev4_ref[c, i, at, :], store)

            loop(2, layer)


    for t in range(tiles + 1):
        lanes = pl.ds(t * LANES, LANES)
        side = t == tiles
        stiff = stiff4_ref[...] if side else stiff_ref[:, lanes]
        for c in range(3):
            ghost = ghost4_ref[c] if side else ghost_ref[c, :, lanes]
            first, second = [edge_ref[c, i] if side else step_ref[c, edge_k + i, :, lanes] for i in range(2)]
            plane_ref[c, :, lanes] = first + second
            plane_ref[3 + c, :, lanes] = stiff * (ghost - first) if stretched else first + ghost
        plane_ref[6, :, lanes] = stiff
    for copy in stores:
        copy.wait()


def wave(
    now, coef, stretch, znow, zcoef, side, zside, low, up, zlow, zup, prev, prev4, ghost, ghost4, stiff, stiff4, edge_k
):
    rows, cols = prev.shape[2:]
    tiles = cols // LANES
    ext = rows + 16
    stretched = zcoef.shape[0] == 3
    vmem = pl.BlockSpec(memory_space=pltpu.VMEM)
    hbm = pl.BlockSpec(memory_space=pl.ANY)
    f32 = jnp.float32
    units = 3 * (10 * (ext - 8) // 8 * (tiles + 1) + rows * tiles)
    return pl.pallas_call(
        functools.partial(wave_kernel, rows, tiles, stretched, edge_k),
        out_shape=(
            jax.ShapeDtypeStruct((3, 8, rows, cols), f32),
            jax.ShapeDtypeStruct((7, rows, cols + LANES), f32),
        ),
        in_specs=[hbm] * 7 + [vmem] * 4 + [hbm] + [vmem] * 6,
        out_specs=(hbm, vmem),
        scratch_shapes=[
            pltpu.VMEM((3, 8, rows, cols), f32),
            pltpu.VMEM((3, 8, rows, cols), f32),
            pltpu.VMEM((3, 2, rows, LANES), f32),
            pltpu.VMEM((3, 16, tiles + 1, ext, LANES), f32),
            pltpu.VMEM((3, 16, tiles + 1, ext, LANES), f32),
            pltpu.VMEM((zcoef.shape[0], 12, tiles + 1, ext, LANES), f32),
            pltpu.VMEM((3, 16, ext, LANES), f32),
            pltpu.VMEM((3, 12, ext, LANES), f32),
            pltpu.VMEM((12, ext, LANES), f32),
            pltpu.VMEM((16, ext, LANES), f32),
            pltpu.VMEM((max(C1, C2) * 6 * ext, 256), jnp.bfloat16),
            pltpu.SemaphoreType.DMA((tiles + 1, 5)),
            pltpu.SemaphoreType.DMA((tiles,)),
        ],
        compiler_params=pltpu.CompilerParams(vmem_limit_bytes=58 * 2**20),
        cost_estimate=pl.CostEstimate(flops=units * 100000, bytes_accessed=10 * 2**20, transcendentals=0),
    )(
        now, coef, stretch, znow, zcoef, side, zside, low, up, zlow, zup, prev, prev4, ghost, ghost4, stiff, stiff4,
        jnp.asarray(derivative_matrix(), jnp.bfloat16),
    )


def slots(widths):
    out, tile, lane = [], 0, 0
    for width in widths:
        if lane + width > LANES:
            tile, lane = tile + 1, 0
        out.append((tile, lane))
        lane += width
    return out, tile + 1


FINE_HALO = ((9, 8), (7, 6), (5, 4), (5, 4), (5, 4))
COARSE_HALO = ((7, 8), (5, 6), (3, 4), (3, 4), (3, 4))


def items_of(halo, n_coef):
    kinds = [0] * 24 + [1] * (8 * n_coef) + [2] * 6 + [3] * 3 + [4]
    halos = [halo[k] for k in kinds]
    places, n_tiles = slots([max(h) for h in halos])
    return halos, places, n_tiles


def lane_between(lane, first, width):
    first = first % LANES
    if first + width <= LANES:
        return (lane >= first) & (lane < first + width)
    return (lane >= first) | (lane < first + width - LANES)


def pack_kernel(*refs):
    fine_in, coarse_in, (low_ref, up_ref) = refs[:14], refs[14:26], refs[26:]
    block = 0
    for rows, ins, halo, n_coef in ((64, fine_in, FINE_HALO, 3), (32, coarse_in, COARSE_HALO, 2)):
        halos, places, n_tiles = items_of(halo, n_coef)
        lane = lax.broadcasted_iota(jnp.int32, (rows, LANES), 1)
        half = lane < 64
        pick = lambda i, *at: jnp.where(half, ins[2 * i][at], ins[2 * i + 1][at])
        scale = 12.0 if n_coef == 3 else 48.0

        def coefficients(z):
            mu, lam = pick(1, z), pick(2, z)
            inverse = 1.0 / (scale * pick(3, z))
            out = [mu * inverse, (mu + lam) * inverse]
            return out + [pick(4, z)] if n_coef == 3 else out

        values = [lambda c=c, z=z: pick(0, c, z) for c in range(3) for z in range(8)]
        held = {}

        def coefficient(c, z):
            if z not in held:
                held[z] = coefficients(z)
            return held[z][c]

        values += [lambda c=c, z=z: coefficient(c, z) for z in range(8) for c in range(n_coef)]
        at = 5 if n_coef == 3 else 4
        values += [lambda c=c, z=z: pick(at, c, z) for c in range(3) for z in range(2)]
        values += [lambda c=c: pick(at + 1, c) for c in range(3)]
        if n_coef == 3:
            values.append(lambda: pick(1, 7) * pick(4, 7))
        else:
            values.append(lambda: 2.0 / pick(1, 0))
        for tile in range(n_tiles):
            low = jnp.zeros((rows, LANES), jnp.float32)
            up = jnp.zeros((rows, LANES), jnp.float32)
            for value, (lo, hi), (home, first) in zip(values, halos, places):
                if home == tile:
                    turned = value()
                    turned = pltpu.roll(turned, first, 1) if first else turned
                    low = jnp.where(lane_between(lane, first, hi), turned, low)
                    up = jnp.where(lane_between(lane, first - lo, lo), turned, up)
            for r in range(rows // 8):
                low_ref[block] = low[8 * r : 8 * r + 8]
                up_ref[block] = up[8 * r : 8 * r + 8]
                block += 1


Y_BLOCKS = 8 * items_of(FINE_HALO, 3)[2] + 4 * items_of(COARSE_HALO, 2)[2]


def pack(fine, coarse):
    specs, operands = [], []
    for arrays, layer_of_prev, tiles in ((fine, 3, 4), (coarse, 0, 2)):
        for i, a in enumerate(arrays):
            block = list(a.shape[:-1]) + [LANES]
            at = [0] * a.ndim
            if i == len(arrays) - 2:
                block[1], at[1] = 2, layer_of_prev
            for tile in (0, tiles - 1):
                where = tuple(at[:-1] + [tile])
                specs.append(pl.BlockSpec(tuple(block), lambda i, where=where: where))
                operands.append(a)
    out = jax.ShapeDtypeStruct((Y_BLOCKS, 8, LANES), jnp.float32)
    whole = pl.BlockSpec((Y_BLOCKS, 8, LANES), lambda i: (0, 0, 0))
    return pl.pallas_call(
        pack_kernel, grid=(1,), out_shape=(out, out), in_specs=specs, out_specs=(whole, whole),
        compiler_params=pltpu.CompilerParams(vmem_limit_bytes=56 * 2**20),
    )(*operands)


def coefficient_kernel(scales, *refs):
    n = len(scales)
    for i, scale in enumerate(scales):
        mu, lam, rho = refs[3 * i : 3 * i + 3]
        out = refs[3 * n + 1 + i]

        def layer(z, carry, mu=mu, lam=lam, rho=rho, out=out, scale=scale):
            inverse = 1.0 / (scale * rho[z])
            out[0, z] = mu[z] * inverse
            out[1, z] = (mu[z] + lam[z]) * inverse
            return carry

        lax.fori_loop(0, 8, layer, 0)
    stretch, stiff, flex = refs[3 * n], refs[-2], refs[-1]
    stiff[...] = refs[0][7] * stretch[0]
    flex[...] = 2.0 / refs[3][0]


def coefficients(fine, coarse, stretch):
    vmem = pl.BlockSpec(memory_space=pltpu.VMEM)
    shapes = [(2,) + a[0].shape for a in (fine, coarse)] + [a[0].shape[1:] for a in (fine, coarse)]
    return pl.pallas_call(
        functools.partial(coefficient_kernel, (12.0, 48.0)),
        out_shape=tuple(jax.ShapeDtypeStruct(a, jnp.float32) for a in shapes),
        in_specs=[vmem] * 7, out_specs=(vmem,) * 4,
        compiler_params=pltpu.CompilerParams(vmem_limit_bytes=56 * 2**20),
        cost_estimate=pl.CostEstimate(flops=10**7, bytes_accessed=7 * 2**20, transcendentals=0),
    )(*fine, *coarse, stretch)


def unpack_kernel(rows, halo, n_coef, block0, *refs):
    from_up, from_low = refs[:2]
    edges, outs, msgs = refs[2:-6], refs[-6:-2], refs[-2:]
    g = lax.axis_index("grid")
    gy = lax.axis_index("gy")
    keep_low, keep_up = gy > 0, gy < lax.axis_size("gy") - 1
    near = near_base(g)
    width = 5 if n_coef == 3 else 3
    if True:
        halos, places, n_tiles = items_of(halo, n_coef)
        lane = lax.broadcasted_iota(jnp.int32, (rows, LANES), 1)
        side_ref, prev_ref, ghost_ref, stiff_ref = outs
        stores = [lambda v, c=c, z=z: side_ref.__setitem__((c, z), v) for c in range(3) for z in range(8)]
        stores += [lambda v, c=c, z=z: side_ref.__setitem__((3 + c, z), v) for z in range(8) for c in range(n_coef)]
        stores += [lambda v, c=c, z=z: prev_ref.__setitem__((c, z), v) for c in range(3) for z in range(2)]
        stores += [lambda v, c=c: ghost_ref.__setitem__((c,), v) for c in range(3)]
        stores += [lambda v: stiff_ref.__setitem__((Ellipsis,), v)]
        tiles = []
        for tile in range(n_tiles):
            at = pl.ds(block0 + tile * rows // 8, rows // 8)
            tiles.append((from_up[at].reshape(rows, LANES), from_low[at].reshape(rows, LANES)))
        block0 += n_tiles * rows // 8
        for store, (lo, hi), (home, first) in zip(stores, halos, places):
            up, low = tiles[home]
            both = jnp.where(lane_between(lane, first, hi), up, low)
            both = pltpu.roll(both, LANES - first, 1) if first else both
            valid = ((lane < hi) & keep_up) | ((lane >= LANES - lo) & keep_low)
            store(jnp.where(valid, both, 0.0))
    if True:
        side_ref = outs[0]
        half_blocks = (6 + n_coef) * width
        first_rows, last_rows = edges[0::2], edges[1::2]
        for msg, edge, is_last in ((msgs[0], first_rows, False), (msgs[1], last_rows, True)):
            for start, layer0 in ((0, near), (half_blocks, 4 - near)):
                for t in range(width):
                    lanes = pl.ds(t * LANES, LANES)

                    def rows_of(kind, c, z, count):
                        if t == width - 1:
                            tile = pl.ds(rows - 8, 8) if is_last else pl.ds(0, 8)
                            v = side_ref[3 * kind + c, z, tile, :]
                        elif kind == 0:
                            v = edge[0][c, z, :, lanes]
                        elif c < 2:
                            v = edge[1][c, z, :, lanes]
                        else:
                            v = edge[2][z, :, lanes]
                        return v[8 - count :] if is_last else v[:count]

                    for c in range(3):
                        for i in range(2):
                            parts = [rows_of(0, c, layer0 + 2 * i + h, 4) for h in range(2)]
                            msg[start + (c * 2 + i) * width + t] = jnp.concatenate(parts, axis=0)
                    for c in range(n_coef):
                        parts = [rows_of(1, c, layer0 + h, 2) for h in range(4)]
                        msg[start + (6 + c) * width + t] = jnp.concatenate(parts, axis=0)


def unpack(from_up, from_low, arrays, halo, block0):
    rows, cols = arrays[0].shape[2:]
    n_coef = len(arrays)
    specs, operands = [], []
    blocks = from_up.shape[0]
    whole = pl.BlockSpec((blocks, 8, LANES), lambda i: (0, 0, 0))
    for a in arrays:
        block = list(a.shape)
        block[-2] = 8
        for tile in (0, rows // 8 - 1):
            where = tuple([0] * (a.ndim - 2) + [tile, 0])
            specs.append(pl.BlockSpec(tuple(block), lambda i, where=where: where))
            operands.append(a)
    shapes = [(3 + n_coef, 8, rows, LANES), (3, 2, rows, LANES), (3, rows, LANES), (rows, LANES)]
    shapes += [(2 * (6 + n_coef) * (cols // LANES + 1), 8, LANES)] * 2
    return pl.pallas_call(
        functools.partial(unpack_kernel, rows, halo, n_coef, block0), grid=(1,),
        out_shape=tuple(jax.ShapeDtypeStruct(s, jnp.float32) for s in shapes),
        in_specs=[whole, whole] + specs,
        out_specs=tuple(pl.BlockSpec(s, lambda i, n=len(s): (0,) * n) for s in shapes),
        compiler_params=pltpu.CompilerParams(vmem_limit_bytes=56 * 2**20),
        cost_estimate=pl.CostEstimate(flops=rows * 10**5, bytes_accessed=rows * 2**16, transcendentals=0),
    )(from_up, from_low, *operands)


def ring(value, axis, by):
    n = lax.axis_size(axis)
    return lax.ppermute(value, axis, [(i, (i + by) % n) for i in range(n)])


def swap(value):
    return lax.ppermute(value, "grid", [(0, 1), (1, 0)])


def neighbours(pieces, axis):
    n = lax.axis_size(axis)
    index = lax.axis_index(axis)
    lows = [lax.slice_in_dim(a, a.shape[d] - lo, a.shape[d], axis=d) for a, d, lo, up in pieces]
    ups = [lax.slice_in_dim(a, 0, up, axis=d) for a, d, lo, up in pieces]

    def move(parts, by, keep):
        flat = jnp.concatenate([p.reshape(-1) for p in parts])
        flat = jnp.pad(flat, (0, -flat.size % 1024)).reshape(-1, LANES)
        flat = jnp.where(keep, ring(flat, axis, by), 0.0).reshape(-1)
        out, at = [], 0
        for p in parts:
            out.append(lax.slice_in_dim(flat, at, at + p.size).reshape(p.shape))
            at += p.size
        return out

    return list(zip(move(lows, 1, index > 0), move(ups, -1, index < n - 1)))


def prolong_matrix(m_rows, m_at, x_rows, x_at):
    out = np.zeros((x_rows, m_rows), np.float32)
    where = {m_at(j): j for j in range(m_rows)}
    for i in range(x_rows):
        x = x_at(i)
        m = x // 2
        weights = {m: 1.0} if x % 2 == 0 else {m - 1: -1 / 16, m: 9 / 16, m + 1: 9 / 16, m + 2: -1 / 16}
        for target, weight in weights.items():
            if target in where:
                out[i, where[target]] = weight
    return out


def restrict_matrix(m_rows, m_at, x_rows, x_at):
    out = np.zeros((m_rows, x_rows), np.float32)
    where = {x_at(i): i for i in range(x_rows)}
    for j in range(m_rows):
        m = m_at(j)
        for target, weight in {2 * m - 1: 0.25, 2 * m: 0.5, 2 * m + 1: 0.25}.items():
            if target in where:
                out[j, where[target]] = weight
    return out


def times(rows, w_ref):
    n = rows.shape[0]
    high = rows.astype(jnp.bfloat16)
    low = (rows - high.astype(jnp.float32)).astype(jnp.bfloat16)
    out = jnp.dot(jnp.concatenate([high, low], axis=0), w_ref[...], preferred_element_type=jnp.float32)
    return out[:n] + out[n:]


def interface_kernel(*refs):
    fine, coarse, (py_ref, ry_ref) = refs[0:6], refs[6:12], refs[12:14]
    (out_fine, out_coarse, fine_plane, coarse_plane, tall, short, sem) = refs[16:]
    g = lax.axis_index("grid")
    gx = lax.axis_index("gx")
    lower = g == 1
    keep_low, keep_up = gx > 0, gx < lax.axis_size("gx") - 1
    fine_rows, coarse_rows = tall.shape[1] - 16, short.shape[1]
    half = fine_rows // 2

    def grown(parts, i, own):
        core, low, up = [jnp.where(own, parts[k][i], parts[3 + k][i]) for k in range(3)]
        return jnp.concatenate([jnp.where(keep_low, low, 0.0), core, jnp.where(keep_up, up, 0.0)], axis=0)

    def prolong(planes):
        whole = []
        for plane in planes:
            parts = []
            for t in range(plane.shape[1] // LANES):
                short[t] = plane[:, t * LANES : (t + 1) * LANES]
                at = lambda i: short[t, pl.ds(i, half), :]
                tall[t, pl.ds(0, half, stride=2), :] = at(4)
                tall[t, pl.ds(1, half, stride=2), :] = (9.0 * (at(4) + at(5)) - (at(3) + at(6))) * 0.0625
                parts.append(tall[t, pl.ds(0, fine_rows), :])
            whole.append(jnp.concatenate(parts, axis=1))
        out = times(jnp.concatenate(whole, axis=0), py_ref)
        return [out[c * fine_rows : (c + 1) * fine_rows] for c in range(3)]

    def restrict(planes):
        whole = []
        for plane in planes:
            parts = []
            for t in range(plane.shape[1] // LANES):
                tall[t, pl.ds(8, fine_rows), :] = plane[:, t * LANES : (t + 1) * LANES]
                at = lambda i: tall[t, pl.ds(i, half, stride=2), :]
                parts.append(0.25 * (at(7) + at(9)) + 0.5 * at(8))
            whole.append(jnp.concatenate(parts, axis=1))
        out = times(jnp.concatenate(whole, axis=0), ry_ref)
        gap = jnp.zeros((4, out.shape[1]), jnp.float32)
        return [jnp.concatenate([gap, out[c * half : (c + 1) * half], gap], axis=0) for c in range(3)]

    tall[...] = jnp.zeros(tall.shape, jnp.float32)
    own_coarse = jnp.logical_not(lower)
    s, f = grown(fine, 6, lower), grown(coarse, 6, own_coarse)
    u, w = [[grown(fine, 3 * k + c, lower) for c in range(3)] for k in range(2)]
    p, q = [[grown(coarse, 3 * k + c, own_coarse) for c in range(3)] for k in range(2)]
    r = restrict(w)
    start = [jnp.where(lower, q[c], p[c] - r[c] * f) for c in range(3)]
    v = prolong(start)
    r = restrict([s * (v[c] - u[c]) for c in range(3)])
    end = [p[c] - r[c] * f for c in range(3)]
    v = prolong(end)
    for c in range(3):
        coarse_plane[c] = end[c][8:-8, : coarse_plane.shape[2]]
        fine_plane[c] = v[c][8:-8, : fine_plane.shape[2]]

    @pl.when(lower)
    def _():
        copy = pltpu.make_async_copy(fine_plane, out_fine.at[:, 7], sem)
        copy.start()
        copy.wait()

    @pl.when(g == 0)
    def _():
        copy = pltpu.make_async_copy(coarse_plane, out_coarse.at[:, 0], sem)
        copy.start()
        copy.wait()


def interface(fine, coarse, fine_step, coarse_step):
    fine_rows, fine_cols = fine[0].shape[1] + 16, fine[0].shape[2]
    coarse_rows, coarse_cols = coarse[0].shape[1] + 16, coarse[0].shape[2]
    cyclic = lambda n: lambda i: i if i < n - LANES // 2 else i - n
    cols = (coarse_cols, cyclic(coarse_cols), fine_cols, cyclic(fine_cols))
    maps = (prolong_matrix(*cols).T, restrict_matrix(*cols).T)
    vmem = pl.BlockSpec(memory_space=pltpu.VMEM)
    hbm = pl.BlockSpec(memory_space=pl.ANY)
    f32 = jnp.float32
    return pl.pallas_call(
        interface_kernel,
        out_shape=tuple(jax.ShapeDtypeStruct(a.shape, f32) for a in (fine_step, coarse_step)),
        in_specs=[vmem] * 14 + [hbm] * 2,
        out_specs=(hbm, hbm),
        input_output_aliases={14: 0, 15: 1},
        scratch_shapes=[
            pltpu.VMEM((3, fine_rows - 16, fine_cols - LANES), f32),
            pltpu.VMEM((3, coarse_rows - 16, coarse_cols - LANES), f32),
            pltpu.VMEM((fine_cols // LANES, fine_rows + 16, LANES), f32),
            pltpu.VMEM((coarse_cols // LANES, coarse_rows, LANES), f32),
            pltpu.SemaphoreType.DMA,
        ],
        compiler_params=pltpu.CompilerParams(vmem_limit_bytes=56 * 2**20),
    )(*fine, *coarse, *[jnp.asarray(m, jnp.bfloat16) for m in maps], fine_step, coarse_step)


def body(
    fine_now, fine_prev, fine_mu, fine_lam, fine_rho, fine_stretch,
    coarse_now, coarse_prev, coarse_mu, coarse_lam, coarse_rho, fine_ghost, coarse_ghost,
):
    g = lax.axis_index("grid")
    low, up = pack(
        (fine_now, fine_mu, fine_lam, fine_rho, fine_stretch, fine_prev, fine_ghost),
        (coarse_now, coarse_mu, coarse_lam, coarse_rho, coarse_prev, coarse_ghost),
    )
    fine_now_z, coarse_now_z, low, up = lax.optimization_barrier((fine_now, coarse_now, low, up))
    from_up, from_low = ring(low, "gy", -1), ring(up, "gy", 1)
    fine_coef, coarse_coef, stiff, flex = coefficients(
        (fine_mu, fine_lam, fine_rho), (coarse_mu, coarse_lam, coarse_rho), fine_stretch[7:]
    )
    cut = lambda a, start, size: lax.dynamic_slice_in_dim(a, start, size, axis=1)
    near = near_base(g)
    near_c = 6 * (1 - g)
    fine_z = swap(cut(fine_now_z, near, 4)), swap(cut(jnp.concatenate([fine_coef, fine_stretch[None]]), near_c, 2))
    coarse_z = swap(cut(coarse_now_z, near, 4)), swap(cut(coarse_coef, near_c, 2))
    coarse_side, coarse_p4, coarse_g4, coarse_s4, coarse_low, coarse_up = unpack(
        from_up, from_low, (coarse_now, coarse_coef), COARSE_HALO, 8 * items_of(FINE_HALO, 3)[2]
    )
    fine_side, fine_p4, fine_g4, fine_s4, fine_low, fine_up = unpack(
        from_up, from_low, (fine_now, fine_coef, fine_stretch), FINE_HALO, 0
    )

    def x_rings(low, up):
        return ring(up, "gx", 1), ring(low, "gx", -1)

    def x_halos(from_low, from_up):
        n = from_low.shape[0] // 2
        return from_low, from_up, swap(from_low[:n]), swap(from_up[:n])

    def plane_halos(planes):
        from_low, from_up = ring(planes[:, -8:], "gx", 1), ring(planes[:, :8], "gx", -1)
        return planes, from_low, from_up, swap(planes), swap(from_low), swap(from_up)

    coarse_x, fine_x = x_rings(coarse_low, coarse_up), x_rings(fine_low, fine_up)
    coarse_zside, fine_zside = swap(cut(coarse_side, near, 4)), swap(cut(fine_side, near, 4))
    coarse_step, coarse_planes = wave(
        coarse_now, coarse_coef, coarse_coef[0], *coarse_z, coarse_side, coarse_zside, *x_halos(*coarse_x),
        coarse_prev, coarse_p4, coarse_ghost, coarse_g4, flex, coarse_s4, 0,
    )
    coarse_step, coarse_planes, *fine_x = lax.optimization_barrier((coarse_step, coarse_planes, *fine_x))
    coarse_planes = plane_halos(coarse_planes)
    fine_step, fine_planes = wave(
        fine_now, fine_coef, fine_stretch, *fine_z, fine_side, fine_zside, *x_halos(*fine_x),
        fine_prev, fine_p4, fine_ghost, fine_g4, stiff, fine_s4, 6,
    )
    return interface(plane_halos(fine_planes), coarse_planes, fine_step, coarse_step)


def solution(mesh):
    block = P(None, "grid", "gx", "gy")
    scalar = P("grid", "gx", "gy")
    plane = P(None, "gx", "gy")
    return jax.shard_map(
        body,
        mesh=mesh,
        in_specs=(block, block, scalar, scalar, scalar, scalar, block, block, scalar, scalar, scalar, plane, plane),
        out_specs=(block, block),
        check_vma=False,
    )
```
